32 devices in a mesh: row: 4 (over y, core), pitch: 4 (over z), span: 2 (over x).
Axes of the slice: x: 2, y: 2, z: 4, core: 2. Of those that a mesh axis runs over, the one named last changes fastest.
Arguments:
- outlet: bfloat16 [4, 2, 5, 1024, 4096], P('row', None, None, 'span', 'pitch'), may hold values from -6 to 6
- remap_weight: bfloat16 [1024, 896], P('span'), may hold values from -0.4375 to 0.4375
- band_start: int32 [896], replicated, may hold values from 0 to 832, as said below
- blade_counts: int32 [2], replicated, may hold values from 12 to 60
- mode_orders: int32 [64, 2], replicated, may hold values from -4 to 4
Outputs:
- stator_inlet: bfloat16 [4, 2, 5, 896, 4096], P('row', None, None, 'span', 'pitch')
The draws below stay inside these ranges and needn't reach their ends.
Inputs may be any that keep to these rules, and one draw needn't show every extreme that they name: Stator radial row m draws from rotor radial rows band_start[m] to band_start[m] + 191; band_start[m] lies within 6 rows of m * 832 / 895, band_start[0] = 0 and band_start[895] = 832.
All inputs are finite; a program needn't handle non-finite values.
Results may differ from the reference program's by a relative error of at most 0.0068.
Values may be sent and summed in bfloat16 or wider, within the bound.
No kernel may reach another device: no remote copies, remote signals or barrier semaphores. Data moves between devices by JAX's collectives and lax.ppermute only.
A program may use at most 64 MiB of HBM per device.

```python
import math
import jax
import jax.numpy as jnp
from jax import lax

R = 1024
RS = 896
PITCH = 4096
HARM = 64
FIELDS = 5
BAND = 192
INST_DEV = 2
ROWS = 4
NTIME = 8


def draw_band_start(key, part):
    stator_rows = jnp.arange(RS, dtype=jnp.int32)
    centred = stator_rows * (R - BAND) // (RS - 1)
    jitter = jax.random.randint(key, (RS,), -6, 7, dtype=jnp.int32)
    starts = jnp.clip(centred + jitter, 0, R - BAND)
    starts = jnp.where(stator_rows == 0, 0, jnp.where(stator_rows == RS - 1, R - BAND, starts))
    return starts.astype(jnp.int32)


def with_ends(array, rng, low, top_value):
    longest = array.shape.index(max(array.shape))
    spots = []
    for shift in (0, 1):
        where = [jax.random.randint(jax.random.fold_in(rng, axis), (), 0, length) for axis, length in enumerate(array.shape)]
        where[longest] = (where[longest] + shift) % array.shape[longest]
        spots.append(tuple(where))
    return array.at[spots[0]].set(low).at[spots[1]].set(top_value)


def steps_of(key, extent, shards, least, top_value):
    level = 1.0
    for dim, blocks in shards:
        heights = jax.random.uniform(jax.random.fold_in(jax.random.fold_in(key, 6), dim), (blocks,), jnp.float32, least / len(shards), top_value / len(shards))
        level = level * jnp.repeat(jnp.exp(heights), extent[dim] // blocks).reshape((-1,) + (1,) * (len(extent) - 1 - dim))
    return level


def bell_draw(stream_key, shape, scale, limit, cuts=(), held_as=jnp.bfloat16):
    drawn = jax.random.normal(stream_key, shape, jnp.float32) * scale
    if len(cuts) > 0:
        drawn = steps_of(stream_key, shape, cuts, -0.22, 0.18) * drawn
    return jnp.clip(drawn, min=-limit, max=limit).astype(held_as)


def setup_inputs(seed: int = 0) -> dict:
    key_list = jax.random.split(jax.random.key(seed), 6)
    return {
        "outlet": bell_draw(key_list[0], (ROWS, INST_DEV, FIELDS, R, PITCH), 1.0, 6.0, ((0, 4), (3, 2), (4, 4))),
        "remap_weight": bell_draw(key_list[1], (R, RS), BAND ** -0.5, 0.4375, ((0, 2),)),
        "band_start": draw_band_start(jax.random.fold_in(key_list[5], 71), 0),
        "blade_counts": jax.random.randint(key_list[3], (2,), 12, 61).astype(jnp.int32),
        "mode_orders": with_ends(jax.random.randint(key_list[4], (HARM, 2), -4, 5), jax.random.fold_in(key_list[4], 1), -4, 4).astype(jnp.int32),
    }


def pitch_table(wavenumber, first_row, number, total_pitch):
    circumferential_coordinates = first_row + jnp.arange(number, dtype=jnp.int32)
    angular_offsets = jnp.mod(circumferential_coordinates[:, None] * wavenumber[None, :], total_pitch)
    angles = 2.0 * math.pi / total_pitch * angular_offsets.astype(jnp.float32)
    return jnp.stack([jnp.cos(angles), jnp.sin(angles)], axis=2).reshape(number, 2 * wavenumber.shape[0])

def reference(outlet, remap_weight, band_start, blade_counts, mode_orders):
    wavenumber = mode_orders[:, 0] * blade_counts[0] + mode_orders[:, 1] * blade_counts[1]
    raw_table = pitch_table(wavenumber, 0, PITCH, PITCH)
    analysis = (raw_table * math.sqrt(2.0 / PITCH)).astype(jnp.bfloat16)
    synthesis = (raw_table * (1.0 / math.sqrt(HARM))).astype(jnp.bfloat16)
    radial_rows = jnp.arange(R, dtype=jnp.int32)
    in_band = (radial_rows[:, None] >= band_start[None, :]) & (radial_rows[:, None] < band_start[None, :] + BAND)
    banded_t = jnp.where(in_band, remap_weight, jnp.zeros_like(remap_weight)).T
    vane_passing_interval = NTIME * blade_counts[0]

    def single_plane(plane_index):
        target_row = plane_index // INST_DEV
        within = plane_index % INST_DEV
        source_row = (target_row + ROWS // 2) % ROWS
        slab_plane = lax.dynamic_index_in_dim(lax.dynamic_index_in_dim(outlet, source_row, 0, False), within, 0, False)
        moment_value = source_row * INST_DEV + within
        spectra = jnp.dot(slab_plane.reshape(FIELDS * R, PITCH), analysis, preferred_element_type=jnp.float32)
        angular_offsets = jnp.mod(wavenumber * moment_value, vane_passing_interval)
        angles = 2.0 * math.pi * angular_offsets.astype(jnp.float32) / vane_passing_interval.astype(jnp.float32)
        cosine = jnp.cos(angles)
        sine_part = jnp.sin(angles)
        paired = spectra.reshape(FIELDS * R, HARM, 2)
        cos_part = paired[:, :, 0]
        sin_part = paired[:, :, 1]
        rotated = jnp.stack([cos_part * cosine - sin_part * sine_part, cos_part * sine_part + sin_part * cosine], axis=2)
        rotated = rotated.reshape(FIELDS, R, 2 * HARM).astype(jnp.bfloat16)
        by_radius = jnp.transpose(rotated, (1, 0, 2)).reshape(R, FIELDS * 2 * HARM)
        remapped = jnp.dot(banded_t, by_radius, preferred_element_type=jnp.float32).astype(jnp.bfloat16)
        by_field = jnp.transpose(remapped.reshape(RS, FIELDS, 2 * HARM), (1, 0, 2)).reshape(FIELDS * RS, 2 * HARM)
        inlet_rows = jnp.dot(by_field, synthesis.T, preferred_element_type=jnp.float32).astype(jnp.bfloat16)
        return inlet_rows.reshape(FIELDS, RS, PITCH)
    results = lax.map(single_plane, jnp.arange(ROWS * INST_DEV, dtype=jnp.int32))
    return results.reshape(ROWS, INST_DEV, FIELDS, RS, PITCH)
```

```python
import functools
import math

import jax
import jax.numpy as jnp
from jax import lax
from jax.experimental import pallas as pl
from jax.experimental.pallas import tpu as pltpu
from jax.sharding import PartitionSpec as P

BAND = 192
JITTER = 6
VMEM_BYTES = 48 * 1024 * 1024
PARTS = 2


def exchange(value, axis, distance):
    count = lax.axis_size(axis)
    return lax.ppermute(value, axis, [(i, i ^ distance) for i in range(count)])


def column_wavenumbers(counts_ref, orders_ref):
    harmonics = orders_ref.shape[1]
    columns = 2 * harmonics
    spread = (
        lax.broadcasted_iota(jnp.int32, (harmonics, columns), 1) // 2
        == lax.broadcasted_iota(jnp.int32, (harmonics, columns), 0)
    )
    orders = jnp.dot(
        orders_ref[...].astype(jnp.float32),
        spread.astype(jnp.float32),
        preferred_element_type=jnp.float32,
    ).astype(jnp.int32)
    return orders[0:1] * counts_ref[0] + orders[1:2] * counts_ref[1]


def table_factors(wave, first_row, rows, total_pitch, turn):
    fine = 32
    coarse = rows // fine
    columns = wave.shape[1]
    step = 2.0 * math.pi / total_pitch
    at_coarse = first_row + fine * lax.broadcasted_iota(jnp.int32, (coarse, columns), 0)
    at_fine = lax.broadcasted_iota(jnp.int32, (fine, columns), 0)
    odd = lax.broadcasted_iota(jnp.int32, (fine, columns), 1) % 2
    q_coarse = lax.rem(at_coarse * wave, total_pitch)
    q_fine = lax.rem(at_fine * wave - odd * (total_pitch // 4), total_pitch)
    a = step * q_coarse.astype(jnp.float32)
    b = step * q_fine.astype(jnp.float32) + turn
    return jnp.cos(a), jnp.sin(a), jnp.cos(b), jnp.sin(b)


def fill_table(ref, at, factors, scale):
    cos_a, sin_a, cos_b, sin_b = factors
    fine = cos_b.shape[0]
    cos_b = cos_b * scale
    sin_b = sin_b * scale
    for i in range(cos_a.shape[0]):
        value = cos_a[i : i + 1] * cos_b - sin_a[i : i + 1] * sin_b
        ref[at + (pl.ds(i * fine, fine), slice(None))] = value.astype(ref.dtype)


def masked_weights(weight, band_start, first_row):
    rows = first_row + lax.broadcasted_iota(jnp.int32, weight.shape, 0)
    inside = (rows >= band_start) & (rows < band_start + BAND)
    return jnp.where(inside, weight.astype(jnp.float32), 0.0)


def edge_kernel(
    sizes,
    counts_ref,
    orders_ref,
    starts_ref,
    weight_ref,
    planes_ref,
    *rest,
):
    parts, instances, fields, edge, halo, pitch_count, row_count, total_pitch = sizes
    halo_refs = rest[:parts]
    table_ref, edge_ref, edge_weight, flipped, planes_sem, weight_sem = rest[parts:]
    count, rows, pitch = planes_ref.shape
    span_at = lax.axis_index("span")
    rs_loc = weight_ref.shape[1] // 2
    first = pl.multiple_of((1 - span_at) * (rows - edge), 16)
    fetch = [
        pltpu.make_async_copy(
            planes_ref.at[pl.ds(j * fields, fields), pl.ds(first, edge), :],
            edge_ref.at[pl.ds(j * fields, fields)],
            planes_sem.at[j],
        )
        for j in range(instances)
    ]
    fetch_weight = pltpu.make_async_copy(
        weight_ref.at[pl.ds(first, edge), :], edge_weight, weight_sem
    )
    fetch_weight.start()
    for copy in fetch:
        copy.start()
    wave = column_wavenumbers(counts_ref, orders_ref)
    first_instance = lax.axis_index("row") * instances
    period = row_count * instances * counts_ref[0]
    scale = math.sqrt(2.0 / total_pitch)
    for j in range(instances):
        turned = (wave * (first_instance + j)).astype(jnp.float32)
        whole = period.astype(jnp.float32)
        turn = (2.0 * math.pi) * (turned - whole * jnp.floor(turned / whole)) / whole
        factors = table_factors(wave, lax.axis_index("pitch") * pitch, pitch, total_pitch, turn)
        fill_table(table_ref, (j,), factors, scale)
    fetch_weight.wait()
    masked = masked_weights(edge_weight[...], starts_ref[...], span_at * rows + first)
    flipped[...] = masked.T.astype(flipped.dtype)
    halo_first = pl.multiple_of(jnp.where(span_at == 0, rs_loc, rs_loc - halo), 16)
    weights = flipped[pl.ds(halo_first, halo), :]
    per = count // parts
    for j in range(instances):
        fetch[j].wait()
        spectra = jnp.dot(
            edge_ref[pl.ds(j * fields, fields)].reshape(fields * edge, pitch),
            table_ref[j],
            preferred_element_type=jnp.float32,
        ).astype(jnp.bfloat16)
        for f in range(fields):
            at = j * fields + f
            halo_refs[at // per][at % per] = jnp.dot(
                weights,
                spectra[f * edge : (f + 1) * edge],
                preferred_element_type=jnp.float32,
            ).astype(jnp.bfloat16)


def edge_call(sizes, counts, orders, starts, weight, planes):
    parts, instances, fields, edge, halo = sizes[:5]
    count, rows, pitch = planes.shape
    columns = 2 * orders.shape[1]
    vmem = pl.BlockSpec(memory_space=pltpu.VMEM)
    anywhere = pl.BlockSpec(memory_space=pl.ANY)
    return pl.pallas_call(
        functools.partial(edge_kernel, sizes),
        out_shape=[jax.ShapeDtypeStruct((count // parts, halo, columns), jnp.bfloat16)] * parts
        + [jax.ShapeDtypeStruct((instances, pitch, columns), jnp.bfloat16)],
        in_specs=[pl.BlockSpec(memory_space=pltpu.SMEM), vmem, vmem, anywhere, anywhere],
        out_specs=[vmem] * (parts + 1),
        scratch_shapes=[
            pltpu.VMEM((count, edge, pitch), jnp.bfloat16),
            pltpu.VMEM((edge, weight.shape[1]), jnp.bfloat16),
            pltpu.VMEM((weight.shape[1], edge), jnp.bfloat16),
            pltpu.SemaphoreType.DMA((instances,)),
            pltpu.SemaphoreType.DMA,
        ],
        compiler_params=pltpu.CompilerParams(vmem_limit_bytes=VMEM_BYTES),
        cost_estimate=pl.CostEstimate(
            flops=2 * count * edge * columns * (pitch + halo),
            bytes_accessed=2 * count * edge * pitch,
            transcendentals=0,
        ),
        name="edge",
    )(counts, orders, starts, weight, planes)


def band_kernel(starts_ref, weight_ref, band_ref, flipped):
    rows = weight_ref.shape[0]
    shards, per, _ = band_ref.shape
    span_at = lax.axis_index("span")
    pitch_at = lax.axis_index("pitch")
    masked = masked_weights(weight_ref[...], starts_ref[...], span_at * rows)
    flipped[...] = masked.T.astype(flipped.dtype)
    for k in range(shards):
        at = jnp.bitwise_xor(pitch_at, k) if shards > 1 else 0
        first = pl.multiple_of(span_at * (shards * per) + at * per, 16)
        band_ref[k] = flipped[pl.ds(first, per), :]


def band_call(shards, starts, weight):
    rows, stator_rows = weight.shape
    per = stator_rows // 2 // shards
    vmem = pl.BlockSpec(memory_space=pltpu.VMEM)
    return pl.pallas_call(
        band_kernel,
        out_shape=jax.ShapeDtypeStruct((shards, per, rows), jnp.bfloat16),
        in_specs=[vmem, vmem],
        out_specs=vmem,
        scratch_shapes=[pltpu.VMEM((stator_rows, rows), jnp.bfloat16)],
        compiler_params=pltpu.CompilerParams(vmem_limit_bytes=VMEM_BYTES),
        name="band",
    )(starts, weight)


def analyse_kernel(shards, planes_ref, table_ref, band_ref, *out_refs):
    spectra = jnp.dot(
        planes_ref[0], table_ref[0], preferred_element_type=jnp.float32
    ).astype(jnp.bfloat16)
    rows = band_ref.shape[0] // shards
    result = jnp.dot(band_ref[...], spectra, preferred_element_type=jnp.float32)
    for k in range(shards):
        out_refs[k][0] = result[k * rows : (k + 1) * rows].astype(out_refs[k].dtype)


def analyse_call(shards, first, number, fields, planes, table, band):
    count, rows, pitch = planes.shape
    columns = table.shape[2]
    stator = band.shape[0]
    per = stator // shards
    kinds = [jnp.bfloat16 if k % 2 else jnp.float32 for k in range(shards)]
    return pl.pallas_call(
        functools.partial(analyse_kernel, shards),
        grid=(number,),
        out_shape=[jax.ShapeDtypeStruct((number, per, columns), kind) for kind in kinds],
        in_specs=[
            pl.BlockSpec((1, rows, pitch), lambda i: (first + i, 0, 0)),
            pl.BlockSpec((1, pitch, columns), lambda i: ((first + i) // fields, 0, 0)),
            pl.BlockSpec((stator, rows), lambda i: (0, 0)),
        ],
        out_specs=[pl.BlockSpec((1, per, columns), lambda i: (i, 0, 0))] * shards,
        compiler_params=pltpu.CompilerParams(vmem_limit_bytes=VMEM_BYTES),
        cost_estimate=pl.CostEstimate(
            flops=2 * number * rows * columns * (pitch + stator),
            bytes_accessed=2 * number * rows * pitch,
            transcendentals=0,
        ),
        name="analyse",
    )(planes, table, band)


def synthesis_table_kernel(total_pitch, harmonics, counts_ref, orders_ref, table_ref):
    wave = column_wavenumbers(counts_ref, orders_ref)
    rows = table_ref.shape[0]
    factors = table_factors(wave, lax.axis_index("pitch") * rows, rows, total_pitch, 0.0)
    fill_table(table_ref, (), factors, 1.0 / math.sqrt(harmonics))


def synthesis_table(pitch, total_pitch, counts, orders):
    columns = 2 * orders.shape[1]
    vmem = pl.BlockSpec(memory_space=pltpu.VMEM)
    return pl.pallas_call(
        functools.partial(synthesis_table_kernel, total_pitch, orders.shape[1]),
        out_shape=jax.ShapeDtypeStruct((pitch, columns), jnp.bfloat16),
        in_specs=[pl.BlockSpec(memory_space=pltpu.SMEM), vmem],
        out_specs=vmem,
        name="synthesis_table",
    )(counts, orders)


def synthesise_kernel(shards, table_ref, *rest):
    shard_refs = rest[:shards]
    out_ref, gathered = rest[-2:]
    per = shard_refs[0].shape[1]
    pitch_at = lax.axis_index("pitch")
    for k in range(shards):
        at = jnp.bitwise_xor(pitch_at, k) if shards > 1 else 0
        gathered[pl.ds(pl.multiple_of(at * per, 16), per), :] = shard_refs[k][0]
    out_ref[0] = lax.dot_general(
        gathered[...], table_ref[...], (((1,), (1,)), ((), ())), preferred_element_type=jnp.float32
    ).astype(out_ref.dtype)


def synthesise_call(first, count, table, shards, base):
    pitch, columns = table.shape
    number, per, _ = shards[0].shape
    stator = per * len(shards)
    block = pl.BlockSpec((1, per, columns), lambda i: (i, 0, 0))
    operands = [table, *shards]
    in_specs = [pl.BlockSpec((pitch, columns), lambda i: (0, 0))] + [block] * len(shards)
    aliases = {}
    if base is not None:
        aliases = {len(operands): 0}
        operands.append(base)
        in_specs.append(pl.BlockSpec(memory_space=pl.ANY))
    return pl.pallas_call(
        functools.partial(synthesise_kernel, len(shards)),
        grid=(number,),
        out_shape=jax.ShapeDtypeStruct((count, stator, pitch), jnp.bfloat16),
        in_specs=in_specs,
        out_specs=pl.BlockSpec((1, stator, pitch), lambda i: (first + i, 0, 0)),
        scratch_shapes=[pltpu.VMEM((stator, columns), jnp.bfloat16)],
        input_output_aliases=aliases,
        compiler_params=pltpu.CompilerParams(vmem_limit_bytes=VMEM_BYTES),
        cost_estimate=pl.CostEstimate(
            flops=2 * number * stator * columns * pitch,
            bytes_accessed=2 * number * stator * pitch,
            transcendentals=0,
        ),
        name="synthesise",
    )(*operands)


def body(outlet, remap_weight, band_start, blade_counts, mode_orders):
    row_count = lax.axis_size("row")
    pitch_count = lax.axis_size("pitch")
    pitch_at = lax.axis_index("pitch")
    span_at = lax.axis_index("span")
    instances, fields, rows, pitch = outlet.shape[1:]
    stator_rows = remap_weight.shape[1]
    total_rows = rows * 2
    total_pitch = pitch * pitch_count
    rs_loc = stator_rows // 2
    count = instances * fields
    slope = (stator_rows - 1) / (total_rows - BAND)
    above = math.floor((rows - 1 + JITTER) * slope) + 1 - rs_loc
    below = rs_loc - math.ceil((rows - BAND + 1 - JITTER) * slope)
    halo = -(-max(above, below) // 16) * 16
    reach = max(
        rows - math.floor(rs_loc / slope - JITTER),
        math.floor((rs_loc - 1) / slope + JITTER) + BAND - rows,
    )
    edge = -(-reach // 128) * 128
    by_shards = (
        pitch_count & (pitch_count - 1) == 0
        and pitch_count > 1
        and rs_loc % (16 * pitch_count) == 0
        and halo == rs_loc // pitch_count
    )
    shards = pitch_count if by_shards else 1
    parts = PARTS if count % PARTS == 0 else 1
    per_part = count // parts

    planes = outlet.reshape(count, rows, pitch)
    orders = mode_orders.T
    starts = band_start.reshape(1, stator_rows)
    sizes = (parts, instances, fields, edge, halo, pitch_count, row_count, total_pitch)
    *halos, table = edge_call(sizes, blade_counts, orders, starts, remap_weight, planes)
    halos = [exchange(value, "span", 1) for value in halos]
    band = band_call(shards, starts, remap_weight).reshape(rs_loc, rows)
    synthesis = synthesis_table(pitch, total_pitch, blade_counts, orders)
    shift = row_count // 2
    joined = None
    for part in range(parts):
        first = part * per_part
        own = analyse_call(shards, first, per_part, fields, planes, table, band)
        from_span = halos[part].astype(jnp.float32)
        if by_shards:
            halo_at = jnp.where(span_at == 0, pitch_count - 1, 0)

            def with_halo(k, *terms):
                total = jnp.where(jnp.bitwise_xor(pitch_at, k) == halo_at, from_span, 0.0)
                for term in terms:
                    total = total + term.astype(jnp.float32)
                return total.astype(jnp.bfloat16)

            met = {}
            for k in range(2, pitch_count, 2):
                met[k] = exchange(with_halo(k + 1, own[k + 1]), "pitch", 1)
            beside = exchange(with_halo(1, own[1]), "pitch", 1)
            across = [
                exchange(with_halo(k, own[k], met[k]), "pitch", k)
                for k in range(2, pitch_count, 2)
            ]
            total = with_halo(0, own[0], beside, *across)
            held = {}
            for k in range(0, pitch_count, 2):
                pairs = [
                    (g * pitch_count + z, ((g + shift) % row_count) * pitch_count + (z ^ k))
                    for g in range(row_count)
                    for z in range(pitch_count)
                ]
                held[k] = lax.ppermute(total, ("row", "pitch"), pairs)
            for k in range(0, pitch_count, 2):
                held[k + 1] = exchange(held[k], "pitch", 1)
            pieces = [held[k] for k in range(pitch_count)]
        else:
            low = jnp.pad(from_span, ((0, 0), (rs_loc - halo, 0), (0, 0)))
            high = jnp.pad(from_span, ((0, 0), (0, rs_loc - halo), (0, 0)))
            mine = own[0] + jnp.where(span_at == 0, low, high)
            total = lax.psum(mine, "pitch").astype(jnp.bfloat16)
            pairs = [(g, (g + shift) % row_count) for g in range(row_count)]
            pieces = [lax.ppermute(total, "row", pairs)]
        joined = synthesise_call(first, count, synthesis, pieces, joined)
    return joined.reshape(1, instances, fields, rs_loc, pitch)


def solution(mesh):
    placed = (P("row", None, None, "span", "pitch"), P("span", None), P(), P(), P())
    return jax.shard_map(
        body,
        mesh=mesh,
        in_specs=placed,
        out_specs=P("row", None, None, "span", "pitch"),
        check_vma=False,
    )
```

```python
import functools
import math

import jax
import jax.numpy as jnp
from jax import lax
from jax.experimental import pallas as pl
from jax.experimental.pallas import tpu as pltpu
from jax.sharding import PartitionSpec as P

BAND = 192
JITTER = 6
LANES = 128
ORDER = {}
GROUPS = (
    ((0, 0), (0, 1), (0, 2), (0, 3), (1, 0), (1, 2)),
    ((1, 1), (1, 3)),
)
VMEM_BYTES = 32 * 1024 * 1024


def exchange(value, axis, distance):
    count = lax.axis_size(axis)
    return lax.ppermute(value, axis, [(i, i ^ distance) for i in range(count)])


def after(value, *others):
    return lax.optimization_barrier((value, *others))[0] if others else value


def column_wavenumbers(counts_ref, orders_ref):
    harmonics = orders_ref.shape[1]
    columns = 2 * harmonics
    spread = (
        lax.broadcasted_iota(jnp.int32, (harmonics, columns), 1) // 2
        == lax.broadcasted_iota(jnp.int32, (harmonics, columns), 0)
    )
    orders = jnp.dot(
        orders_ref[...].astype(jnp.float32),
        spread.astype(jnp.float32),
        preferred_element_type=jnp.float32,
    ).astype(jnp.int32)
    return orders[0:1] * counts_ref[0] + orders[1:2] * counts_ref[1]


def table_factors(wave, first_row, rows, total_pitch, turn):
    fine = 32
    coarse = rows // fine
    columns = wave.shape[1]
    step = 2.0 * math.pi / total_pitch
    at_coarse = first_row + fine * lax.broadcasted_iota(jnp.int32, (coarse, columns), 0)
    at_fine = lax.broadcasted_iota(jnp.int32, (fine, columns), 0)
    odd = lax.broadcasted_iota(jnp.int32, (fine, columns), 1) % 2
    q_coarse = lax.rem(at_coarse * wave, total_pitch)
    q_fine = lax.rem(at_fine * wave - odd * (total_pitch // 4), total_pitch)
    a = step * q_coarse.astype(jnp.float32)
    b = step * q_fine.astype(jnp.float32) + turn
    return jnp.cos(a), jnp.sin(a), jnp.cos(b), jnp.sin(b)


def fill_table(ref, at, factors, scale):
    cos_a, sin_a, cos_b, sin_b = factors
    fine = cos_b.shape[0]
    cos_b = cos_b * scale
    sin_b = sin_b * scale
    for i in range(cos_a.shape[0]):
        value = cos_a[i : i + 1] * cos_b - sin_a[i : i + 1] * sin_b
        ref[at + (pl.ds(i * fine, fine), slice(None))] = value.astype(ref.dtype)


def geometry(outlet_shape, stator_rows):
    rows = outlet_shape[-2]
    total_rows = 2 * rows
    rs_loc = stator_rows // 2
    slope = (stator_rows - 1) / (total_rows - BAND)
    above = math.floor((rows - 1 + JITTER) * slope) + 1 - rs_loc
    below = rs_loc - math.ceil((rows - BAND + 1 - JITTER) * slope)
    halo = -(-max(above, below) // 16) * 16
    reach = max(
        rows - math.floor(rs_loc / slope - JITTER),
        math.floor((rs_loc - 1) / slope + JITTER) + BAND - rows,
    )
    edge = -(-reach // LANES) * LANES
    return rs_loc, halo, edge


def window(first, number):
    starts = [at // LANES * LANES for at in first]
    width = max(-(-(at + number) // LANES) * LANES - start for at, start in zip(first, starts))
    return starts, width


def by_span(span_at, values, multiple):
    return pl.multiple_of(jnp.where(span_at == 0, values[0], values[1]), multiple)


def flip_weights(weight_ref, starts_ref, first_row, first_column, flipped):
    rows, width = weight_ref.shape
    row = first_row + lax.broadcasted_iota(jnp.int32, (rows, LANES), 0)
    for block in range(width // LANES):
        start = starts_ref[pl.ds(first_column // LANES + block, 1), :]
        inside = (row >= start) & (row < start + BAND)
        at = slice(block * LANES, (block + 1) * LANES)
        value = jnp.where(inside, weight_ref[:, at].astype(jnp.float32), 0.0)
        flipped[at, :] = value.T.astype(flipped.dtype)


def instance_turn(wave, instance, period):
    whole = period.astype(jnp.float32)
    steps = (wave * instance).astype(jnp.float32)
    return (2.0 * math.pi) * (steps - whole * jnp.floor(steps / whole)) / whole


def fill_analysis(wave, counts_ref, part, instances, total_pitch, table_ref):
    pitch = table_ref.shape[0]
    instance = lax.axis_index("row") * instances + part
    period = lax.axis_size("row") * instances * counts_ref[0]
    turn = instance_turn(wave, instance, period)
    factors = table_factors(wave, lax.axis_index("pitch") * pitch, pitch, total_pitch, turn)
    fill_table(table_ref, (), factors, math.sqrt(2.0 / total_pitch))


def started(*copies):
    for copy in copies:
        copy.start()
    return copies


def edge_kernel(
    sizes, counts_hbm, orders_hbm, starts_hbm, weight_hbm, planes_hbm, *rest,
):
    instances, fields, rs_loc, halo, edge, total_pitch = sizes
    halo_refs, (table_ref, planes_ref, mask_ref) = rest[:instances], rest[instances : instances + 3]
    counts, orders, starts, weight, edges, flipped, spectra, sems, plane_sems = rest[
        instances + 3 :
    ]
    rows, pitch = planes_hbm.shape[1:]
    others = rows - edge
    span_at = lax.axis_index("span")
    first_halo = (rs_loc, rs_loc - halo)
    columns, width = window(first_halo, halo)
    first_row = pl.multiple_of((1 - span_at) * (rows - edge), 16)
    first_column = by_span(span_at, columns, LANES)
    small = started(
        pltpu.make_async_copy(counts_hbm, counts, sems.at[0]),
        pltpu.make_async_copy(orders_hbm, orders, sems.at[1]),
        pltpu.make_async_copy(starts_hbm, starts, sems.at[2]),
        pltpu.make_async_copy(
            weight_hbm.at[pl.ds(first_row, edge), pl.ds(first_column, width)], weight, sems.at[3]
        ),
    )
    edge_rows = pl.ds(first_row, edge)
    other_rows = pl.ds(pl.multiple_of(span_at * edge, 16), others)
    fetched = started(
        pltpu.make_async_copy(
            planes_hbm.at[pl.ds(0, fields), edge_rows, :],
            planes_ref.at[:, edge_rows, :],
            plane_sems.at[0],
        ),
        *(
            pltpu.make_async_copy(
                planes_hbm.at[pl.ds(j * fields, fields), edge_rows, :],
                edges.at[j - 1],
                plane_sems.at[j],
            )
            for j in range(1, instances)
        ),
    )
    (rest_fetched,) = started(
        pltpu.make_async_copy(
            planes_hbm.at[pl.ds(0, fields), other_rows, :],
            planes_ref.at[:, other_rows, :],
            plane_sems.at[instances],
        )
    )
    pitch_at = lax.axis_index("pitch")
    for k in range(mask_ref.shape[0]):
        halo_at = jnp.where(span_at == 0, mask_ref.shape[0] - 1, 0)
        at_halo = jnp.bitwise_xor(pitch_at, k) == halo_at
        mask_ref[k] = jnp.full(mask_ref.shape[1:], at_halo.astype(jnp.float32))
    for copy in small[:2]:
        copy.wait()
    wave = column_wavenumbers(counts, orders)
    for j in range(instances):
        fill_analysis(wave, counts, j, instances, total_pitch, table_ref.at[j])
    for copy in small[2:]:
        copy.wait()
    flip_weights(weight, starts, span_at * rows + first_row, first_column, flipped)
    inner = [first - start for first, start in zip(first_halo, columns)]
    weights = flipped[pl.ds(by_span(span_at, inner, 16), halo), :]
    number = table_ref.shape[2]
    for j in range(instances):
        fetched[j].wait()
        taken = planes_ref[:, edge_rows, :] if j == 0 else edges[j - 1]
        result = jnp.dot(
            taken.reshape(fields * edge, pitch),
            table_ref[j],
            preferred_element_type=jnp.float32,
        ).astype(jnp.bfloat16)
        for f in range(fields):
            at = (j * fields + f) * number
            spectra[:, at : at + number] = result[f * edge : (f + 1) * edge]
    result = jnp.dot(weights, spectra[...], preferred_element_type=jnp.float32)
    for j in range(instances):
        for f in range(fields):
            at = (j * fields + f) * number
            halo_refs[j][f] = result[:, at : at + number].astype(jnp.bfloat16)
    rest_fetched.wait()


def edge_call(sizes, shards, counts, orders, starts, weight, planes):
    instances, fields, rs_loc, halo, edge, total_pitch = sizes
    pitch = planes.shape[2]
    columns = 2 * orders.shape[1]
    width = window((rs_loc, rs_loc - halo), halo)[1]
    count = instances * fields
    vmem = pl.BlockSpec(memory_space=pltpu.VMEM)
    hbm = pl.BlockSpec(memory_space=pltpu.HBM)
    return pl.pallas_call(
        functools.partial(edge_kernel, sizes),
        out_shape=[jax.ShapeDtypeStruct((fields, halo, columns), jnp.bfloat16)] * instances
        + [
            jax.ShapeDtypeStruct((instances, pitch, columns), jnp.bfloat16),
            pltpu.VMEM((fields, *planes.shape[1:]), jnp.bfloat16),
            jax.ShapeDtypeStruct((shards, 8, columns), jnp.float32),
        ],
        in_specs=[hbm] * 5,
        out_specs=[vmem] * (instances + 3),
        scratch_shapes=[
            pltpu.SMEM(counts.shape, jnp.int32),
            pltpu.VMEM(orders.shape, jnp.int32),
            pltpu.VMEM(starts.shape, jnp.int32),
            pltpu.VMEM((edge, width), jnp.bfloat16),
            pltpu.VMEM((max(instances - 1, 1), fields, edge, pitch), jnp.bfloat16),
            pltpu.VMEM((width, edge), jnp.bfloat16),
            pltpu.VMEM((edge, count * columns), jnp.bfloat16),
            pltpu.SemaphoreType.DMA((4,)),
            pltpu.SemaphoreType.DMA((instances + 1,)),
        ],
        compiler_params=pltpu.CompilerParams(vmem_limit_bytes=VMEM_BYTES),
        cost_estimate=pl.CostEstimate(
            flops=2 * count * edge * columns * (pitch + halo),
            bytes_accessed=2 * count * edge * pitch,
            transcendentals=0,
        ),
        name="edge",
    )(counts, orders, starts, weight, planes)


def analyse_planes(planes_ref, table_ref, band_ref, spectra, out_refs):
    fields, rows, pitch = planes_ref.shape
    columns = table_ref.shape[1]
    per = band_ref.shape[0] // len(out_refs)
    result = jnp.dot(
        planes_ref[...].reshape(fields * rows, pitch),
        table_ref[...],
        preferred_element_type=jnp.float32,
    ).astype(jnp.bfloat16)
    for f in range(fields):
        spectra[:, f * columns : (f + 1) * columns] = result[f * rows : (f + 1) * rows]
    result = jnp.dot(band_ref[...], spectra[...], preferred_element_type=jnp.float32)
    for k, out_ref in enumerate(out_refs):
        for f in range(fields):
            out_ref[f] = result[
                k * per : (k + 1) * per, f * columns : (f + 1) * columns
            ].astype(out_ref.dtype)


def next_planes(planes_hbm, part, next_ref, sem):
    return pltpu.make_async_copy(
        planes_hbm.at[pl.ds((part + 1) * next_ref.shape[0], next_ref.shape[0])], next_ref, sem
    )


def first_kernel(
    sizes, shards, starts_hbm, weight_hbm, planes_hbm, planes_ref, table_ref, *rest,
):
    instances, fields, rs_loc, halo, edge, total_pitch = sizes
    out_refs, band_ref, next_refs = rest[:shards], rest[shards], rest[shards + 1 : -5]
    starts, weight, flipped, spectra, sems = rest[-5:]
    rows = weight_hbm.shape[0]
    per = rs_loc // shards
    span_at = lax.axis_index("span")
    pitch_at = lax.axis_index("pitch")
    columns, width = window((0, rs_loc), rs_loc)
    first_column = by_span(span_at, columns, LANES)
    small = started(
        pltpu.make_async_copy(starts_hbm, starts, sems.at[0]),
        pltpu.make_async_copy(weight_hbm.at[:, pl.ds(first_column, width)], weight, sems.at[1]),
    )
    following = started(*(next_planes(planes_hbm, 0, ref, sems.at[2]) for ref in next_refs))
    for copy in small:
        copy.wait()
    flip_weights(weight, starts, span_at * rows, first_column, flipped)
    own = by_span(span_at, (0, rs_loc - columns[1]), 16)
    for k in range(shards):
        at = jnp.bitwise_xor(pitch_at, k) if shards > 1 else 0
        source = pl.multiple_of(own + at * per, 16)
        band_ref[k * per : (k + 1) * per] = flipped[pl.ds(source, per), :]
    analyse_planes(planes_ref, table_ref.at[0], band_ref, spectra, out_refs)
    for copy in following:
        copy.wait()


def own_shapes(shards, fields, per, columns):
    kinds = [jnp.bfloat16 if k % 2 else jnp.float32 for k in range(shards)]
    return [jax.ShapeDtypeStruct((fields, per, columns), kind) for kind in kinds]


def first_call(sizes, shards, starts, weight, planes, held, table):
    instances, fields, rs_loc, halo, edge, total_pitch = sizes
    rows, pitch = planes.shape[1:]
    columns = table.shape[2]
    width = window((0, rs_loc), rs_loc)[1]
    vmem = pl.BlockSpec(memory_space=pltpu.VMEM)
    hbm = pl.BlockSpec(memory_space=pltpu.HBM)
    following = [pltpu.VMEM((fields, rows, pitch), jnp.bfloat16)] * (instances > 1)
    return pl.pallas_call(
        functools.partial(first_kernel, sizes, shards),
        out_shape=own_shapes(shards, fields, rs_loc // shards, columns)
        + [jax.ShapeDtypeStruct((rs_loc, rows), jnp.bfloat16)]
        + following,
        in_specs=[hbm, hbm, hbm, vmem, vmem],
        out_specs=[vmem] * (shards + 1 + len(following)),
        scratch_shapes=[
            pltpu.VMEM(starts.shape, jnp.int32),
            pltpu.VMEM((rows, width), jnp.bfloat16),
            pltpu.VMEM((width, rows), jnp.bfloat16),
            pltpu.VMEM((rows, fields * columns), jnp.bfloat16),
            pltpu.SemaphoreType.DMA((3,)),
        ],
        compiler_params=pltpu.CompilerParams(vmem_limit_bytes=VMEM_BYTES),
        cost_estimate=pl.CostEstimate(
            flops=2 * fields * rows * columns * (pitch + rs_loc),
            bytes_accessed=2 * fields * rows * pitch,
            transcendentals=0,
        ),
        name="first_part",
    )(starts, weight, planes, held, table)


def later_kernel(
    sizes, shards, part,
    counts_hbm, orders_hbm, planes_hbm, planes_ref, table_ref, band_ref, after_ref, *rest,
):
    out_refs, synthesis_ref, next_refs = rest[:shards], rest[shards], rest[shards + 1 : -4]
    counts, orders, spectra, sems = rest[-4:]
    small = started(
        pltpu.make_async_copy(counts_hbm, counts, sems.at[0]),
        pltpu.make_async_copy(orders_hbm, orders, sems.at[1]),
    )
    following = started(*(next_planes(planes_hbm, part, ref, sems.at[2]) for ref in next_refs))
    analyse_planes(planes_ref, table_ref.at[part], band_ref, spectra, out_refs)
    for copy in small:
        copy.wait()
    wave = column_wavenumbers(counts, orders)
    pitch = synthesis_ref.shape[0]
    factors = table_factors(wave, lax.axis_index("pitch") * pitch, pitch, sizes[-1], 0.0)
    fill_table(synthesis_ref, (), factors, 1.0 / math.sqrt(wave.shape[1] // 2))
    for copy in following:
        copy.wait()


def later_call(sizes, shards, part, counts, orders, planes, held, table, band, after):
    instances, fields, rs_loc, halo, edge, total_pitch = sizes
    rows, pitch = planes.shape[1:]
    columns = table.shape[2]
    vmem = pl.BlockSpec(memory_space=pltpu.VMEM)
    hbm = pl.BlockSpec(memory_space=pltpu.HBM)
    following = [pltpu.VMEM((fields, rows, pitch), jnp.bfloat16)] * (part + 1 < instances)
    return pl.pallas_call(
        functools.partial(later_kernel, sizes, shards, part),
        out_shape=own_shapes(shards, fields, rs_loc // shards, columns)
        + [jax.ShapeDtypeStruct((pitch, columns), jnp.bfloat16)]
        + following,
        in_specs=[hbm, hbm, hbm, vmem, vmem, vmem, pl.BlockSpec(memory_space=pl.ANY)],
        out_specs=[vmem] * (shards + 1 + len(following)),
        scratch_shapes=[
            pltpu.SMEM(counts.shape, jnp.int32),
            pltpu.VMEM(orders.shape, jnp.int32),
            pltpu.VMEM((rows, fields * columns), jnp.bfloat16),
            pltpu.SemaphoreType.DMA((3,)),
        ],
        compiler_params=pltpu.CompilerParams(vmem_limit_bytes=VMEM_BYTES),
        cost_estimate=pl.CostEstimate(
            flops=2 * fields * rows * columns * (pitch + rs_loc),
            bytes_accessed=2 * fields * rows * pitch,
            transcendentals=0,
        ),
        name="later_part",
    )(counts, orders, planes, held, table, band, after)


def synthesise_kernel(fields, ranks, shards, per, table_ref, *rest):
    piece_refs = rest[: len(ranks)]
    out_hbm, rows_ref, sems = rest[-3:]
    pitch_at = lax.axis_index("pitch")
    copies = []
    for i, (part, k) in enumerate(ranks):
        piece = piece_refs[i][...]
        value = lax.dot_general(
            piece.reshape(fields * per, piece.shape[2]),
            table_ref[...],
            (((1,), (1,)), ((), ())),
            preferred_element_type=jnp.float32,
        )
        rows_ref[i] = value.astype(rows_ref.dtype).reshape(fields, per, value.shape[1])
        at = jnp.bitwise_xor(pitch_at, k) if shards > 1 else 0
        copies += started(
            pltpu.make_async_copy(
                rows_ref.at[i],
                out_hbm.at[
                    pl.ds(part * fields, fields), pl.ds(pl.multiple_of(at * per, 16), per), :
                ],
                sems.at[i],
            )
        )
    for copy in copies:
        copy.wait()


def synthesise_call(count, shards, table, pieces, base):
    ranks = list(pieces)
    fields, per, columns = pieces[ranks[0]].shape
    pitch = table.shape[0]
    vmem = pl.BlockSpec(memory_space=pltpu.VMEM)
    hbm = pl.BlockSpec(memory_space=pltpu.HBM)
    operands = [table, *pieces.values()]
    in_specs = [vmem] * len(operands)
    aliases = {}
    if base is not None:
        aliases = {len(operands): 0}
        operands.append(base)
        in_specs.append(hbm)
    return pl.pallas_call(
        functools.partial(synthesise_kernel, fields, ranks, shards, per),
        out_shape=jax.ShapeDtypeStruct((count, per * shards, pitch), jnp.bfloat16),
        in_specs=in_specs,
        out_specs=hbm,
        scratch_shapes=[
            pltpu.VMEM((len(ranks), fields, per, pitch), jnp.bfloat16),
            pltpu.SemaphoreType.DMA((len(ranks),)),
        ],
        input_output_aliases=aliases,
        compiler_params=pltpu.CompilerParams(vmem_limit_bytes=VMEM_BYTES),
        cost_estimate=pl.CostEstimate(
            flops=2 * len(ranks) * fields * per * columns * pitch,
            bytes_accessed=2 * len(ranks) * fields * per * pitch,
            transcendentals=0,
        ),
        name="synthesise",
    )(*operands)


def body(outlet, remap_weight, band_start, blade_counts, mode_orders):
    row_count = lax.axis_size("row")
    pitch_count = lax.axis_size("pitch")
    instances, fields, rows, pitch = outlet.shape[1:]
    stator_rows = remap_weight.shape[1]
    total_pitch = pitch * pitch_count
    rs_loc, halo_rows, edge = geometry(outlet.shape, stator_rows)
    count = instances * fields
    by_shards = (
        pitch_count == 4
        and rs_loc % (16 * pitch_count) == 0
        and halo_rows == rs_loc // pitch_count
    )
    shards = pitch_count if by_shards else 1
    shift = row_count // 2

    def stay(value):
        return pltpu.with_memory_space_constraint(value, pltpu.HBM)

    planes = stay(outlet.reshape(count, rows, pitch))
    orders = stay(mode_orders.T)
    starts = stay(band_start.reshape(stator_rows // LANES, LANES))
    blade_counts = stay(blade_counts)
    remap_weight = stay(remap_weight)
    sizes = (instances, fields, rs_loc, halo_rows, edge, total_pitch)
    *halos, table, held, masks = edge_call(
        sizes, shards, blade_counts, orders, starts, remap_weight, planes
    )
    made = first_call(sizes, shards, starts, remap_weight, planes, held, table)
    owns, band, held = [made[:shards]], made[shards], made[-1]
    known = {}

    def get(kind, part):
        if (kind, part) not in known:
            known[kind, part] = steps[kind](part)
        return known[kind, part]

    def ready(kind, part, value):
        return after(value, *(get(*step) for step in ORDER.get((kind, part), ())))

    def later(part):
        if part == 0:
            return owns[0][-1]
        first_sent = halos[0] if shards == 1 else get("meet", 0)[1]
        made = later_call(
            sizes, shards, part, blade_counts, orders, planes,
            known.get(("held", part), held), table, band, ready("later", part, first_sent),
        )
        owns.append(made[:shards])
        known["synthesis", 0] = made[shards]
        known["held", part + 1] = made[-1]
        return made[0]

    def halo(part):
        return exchange(ready("halo", part, halos[part]), "span", 1)

    def with_halo(part, k, *terms):
        get("later", part)
        total = jnp.where(masks[k, :1] > 0.0, get("halo", part).astype(jnp.float32), 0.0)
        for term in (owns[part][k], *terms):
            total = total + term.astype(jnp.float32)
        return total.astype(jnp.bfloat16)

    def meet(part):
        return None, with_halo(part, 3)

    def pair(part):
        return exchange(ready("pair", part, get("meet", part)[1]), "pitch", 1)

    def beside(part):
        return exchange(ready("beside", part, with_halo(part, 1)), "pitch", 1)

    def across(part):
        return exchange(
            ready("across", part, with_halo(part, 2, get("pair", part))), "pitch", 2
        )

    def total(part):
        return with_halo(part, 0, get("beside", part), get("across", part))

    def spread(value, k):
        pairs = [
            (g * pitch_count + z, ((g + shift) % row_count) * pitch_count + (z ^ k))
            for g in range(row_count)
            for z in range(pitch_count)
        ]
        return lax.ppermute(value, ("row", "pitch"), pairs)

    def swap(part):
        return spread(ready("swap", part, get("total", part)), 0)

    def swap_across(part):
        return spread(ready("swap_across", part, get("total", part)), 2)

    def swap_on(part):
        return exchange(ready("swap_on", part, get("swap", part)), "pitch", 1)

    def across_on(part):
        return exchange(ready("across_on", part, get("swap_across", part)), "pitch", 1)

    steps = dict(
        later=later, halo=halo, meet=meet, pair=pair, beside=beside, across=across, total=total,
        swap=swap, swap_across=swap_across, swap_on=swap_on, across_on=across_on,
    )
    names = ("swap", "swap_on", "swap_across", "across_on")

    def whole_sum(part):
        get("later", part)
        wide = get("halo", part).astype(jnp.float32)
        low = jnp.pad(wide, ((0, 0), (rs_loc - halo_rows, 0), (0, 0)))
        high = jnp.pad(wide, ((0, 0), (0, rs_loc - halo_rows), (0, 0)))
        mine = owns[part][0] + jnp.where(lax.axis_index("span") == 0, low, high)
        return lax.psum(mine, "pitch").astype(jnp.bfloat16)

    joined = None
    if by_shards:
        for group in GROUPS:
            group = {(part, k): get(names[k], part) for part, k in group}
            joined = synthesise_call(count, shards, known["synthesis", 0], group, joined)
    else:
        pairs = [(g, (g + shift) % row_count) for g in range(row_count)]
        pieces = {
            (part, 0): lax.ppermute(whole_sum(part), "row", pairs) for part in range(instances)
        }
        joined = synthesise_call(count, shards, known["synthesis", 0], pieces, joined)
    return joined.reshape(1, instances, fields, rs_loc, pitch)


def solution(mesh):
    placed = (P("row", None, None, "span", "pitch"), P("span", None), P(), P(), P())
    return jax.shard_map(
        body,
        mesh=mesh,
        in_specs=placed,
        out_specs=P("row", None, None, "span", "pitch"),
        check_vma=False,
    )
```

```python
import functools
import math

import jax
import jax.numpy as jnp
from jax import lax
from jax.experimental import pallas as pl
from jax.experimental.pallas import tpu as pltpu
from jax.sharding import PartitionSpec as P

BAND = 192
JITTER = 6
LANES = 128
ORDER = {}
JOIN = True
DIRECT = True
GROUPS = (((0, 0), (0, 1), (0, 2), (0, 3), (1, 0), (1, 2)), ((1, 1), (1, 3)))
VMEM_BYTES = 32 * 1024 * 1024


def exchange(value, axis, distance):
    count = lax.axis_size(axis)
    return lax.ppermute(value, axis, [(i, i ^ distance) for i in range(count)])


def after(value, *others):
    return lax.optimization_barrier((value, *others))[0] if others else value


def column_wavenumbers(counts_ref, orders_ref):
    harmonics = orders_ref.shape[1]
    columns = 2 * harmonics
    spread = (
        lax.broadcasted_iota(jnp.int32, (harmonics, columns), 1) // 2
        == lax.broadcasted_iota(jnp.int32, (harmonics, columns), 0)
    )
    orders = jnp.dot(
        orders_ref[...].astype(jnp.float32),
        spread.astype(jnp.float32),
        preferred_element_type=jnp.float32,
    ).astype(jnp.int32)
    return orders[0:1] * counts_ref[0] + orders[1:2] * counts_ref[1]


def table_factors(wave, first_row, rows, total_pitch, turn):
    fine = 32
    coarse = rows // fine
    columns = wave.shape[1]
    step = 2.0 * math.pi / total_pitch
    at_coarse = first_row + fine * lax.broadcasted_iota(jnp.int32, (coarse, columns), 0)
    at_fine = lax.broadcasted_iota(jnp.int32, (fine, columns), 0)
    odd = lax.broadcasted_iota(jnp.int32, (fine, columns), 1) % 2
    q_coarse = lax.rem(at_coarse * wave, total_pitch)
    q_fine = lax.rem(at_fine * wave - odd * (total_pitch // 4), total_pitch)
    a = step * q_coarse.astype(jnp.float32)
    b = step * q_fine.astype(jnp.float32) + turn
    return jnp.cos(a), jnp.sin(a), jnp.cos(b), jnp.sin(b)


def fill_table(ref, at, factors, scale):
    cos_a, sin_a, cos_b, sin_b = factors
    fine = cos_b.shape[0]
    cos_b = cos_b * scale
    sin_b = sin_b * scale
    for i in range(cos_a.shape[0]):
        value = cos_a[i : i + 1] * cos_b - sin_a[i : i + 1] * sin_b
        ref[at + (pl.ds(i * fine, fine), slice(None))] = value.astype(ref.dtype)


def geometry(outlet_shape, stator_rows):
    rows = outlet_shape[-2]
    total_rows = 2 * rows
    rs_loc = stator_rows // 2
    slope = (stator_rows - 1) / (total_rows - BAND)
    above = math.floor((rows - 1 + JITTER) * slope) + 1 - rs_loc
    below = rs_loc - math.ceil((rows - BAND + 1 - JITTER) * slope)
    halo = -(-max(above, below) // 16) * 16
    reach = max(
        rows - math.floor(rs_loc / slope - JITTER),
        math.floor((rs_loc - 1) / slope + JITTER) + BAND - rows,
    )
    edge = -(-reach // LANES) * LANES
    return rs_loc, halo, edge


def window(first, number):
    starts = [at // LANES * LANES for at in first]
    width = max(-(-(at + number) // LANES) * LANES - start for at, start in zip(first, starts))
    return starts, width


def by_span(span_at, values, multiple):
    return pl.multiple_of(jnp.where(span_at == 0, values[0], values[1]), multiple)


def flip_weights(weight_ref, starts_ref, first_row, first_column, flipped):
    rows, width = weight_ref.shape
    row = first_row + lax.broadcasted_iota(jnp.int32, (rows, LANES), 0)
    for block in range(width // LANES):
        start = starts_ref[pl.ds(first_column // LANES + block, 1), :]
        inside = (row >= start) & (row < start + BAND)
        at = slice(block * LANES, (block + 1) * LANES)
        value = jnp.where(inside, weight_ref[:, at].astype(jnp.float32), 0.0)
        flipped[at, :] = value.T.astype(flipped.dtype)


def instance_turn(wave, instance, period):
    whole = period.astype(jnp.float32)
    steps = (wave * instance).astype(jnp.float32)
    return (2.0 * math.pi) * (steps - whole * jnp.floor(steps / whole)) / whole


def fill_analysis(wave, counts_ref, part, instances, total_pitch, table_ref):
    pitch = table_ref.shape[0]
    instance = lax.axis_index("row") * instances + part
    period = lax.axis_size("row") * instances * counts_ref[0]
    turn = instance_turn(wave, instance, period)
    factors = table_factors(wave, lax.axis_index("pitch") * pitch, pitch, total_pitch, turn)
    fill_table(table_ref, (), factors, math.sqrt(2.0 / total_pitch))


def started(*copies):
    for copy in copies:
        copy.start()
    return copies


def edge_kernel(
    sizes, counts_hbm, orders_hbm, starts_hbm, weight_hbm, planes_hbm, *rest,
):
    instances, fields, rs_loc, halo, edge, total_pitch = sizes
    halo_refs, (table_ref, planes_ref) = rest[:instances], rest[instances : instances + 2]
    counts, orders, starts, weight, edges, flipped, spectra, sems, plane_sems = rest[
        instances + 2 :
    ]
    rows, pitch = planes_hbm.shape[1:]
    others = rows - edge
    span_at = lax.axis_index("span")
    first_halo = (rs_loc, rs_loc - halo)
    columns, width = window(first_halo, halo)
    first_row = pl.multiple_of((1 - span_at) * (rows - edge), 16)
    first_column = by_span(span_at, columns, LANES)
    small = started(
        pltpu.make_async_copy(counts_hbm, counts, sems.at[0]),
        pltpu.make_async_copy(orders_hbm, orders, sems.at[1]),
        pltpu.make_async_copy(starts_hbm, starts, sems.at[2]),
        pltpu.make_async_copy(
            weight_hbm.at[pl.ds(first_row, edge), pl.ds(first_column, width)], weight, sems.at[3]
        ),
    )
    edge_rows = pl.ds(first_row, edge)
    other_rows = pl.ds(pl.multiple_of(span_at * edge, 16), others)
    fetched = started(
        pltpu.make_async_copy(
            planes_hbm.at[pl.ds(0, fields), edge_rows, :],
            planes_ref.at[:, edge_rows, :],
            plane_sems.at[0],
        ),
        *(
            pltpu.make_async_copy(
                planes_hbm.at[pl.ds(j * fields, fields), edge_rows, :],
                edges.at[j - 1],
                plane_sems.at[j],
            )
            for j in range(1, instances)
        ),
    )
    (rest_fetched,) = started(
        pltpu.make_async_copy(
            planes_hbm.at[pl.ds(0, fields), other_rows, :],
            planes_ref.at[:, other_rows, :],
            plane_sems.at[instances],
        )
    )
    for copy in small[:2]:
        copy.wait()
    wave = column_wavenumbers(counts, orders)
    for j in range(instances):
        fill_analysis(wave, counts, j, instances, total_pitch, table_ref.at[j])
    for copy in small[2:]:
        copy.wait()
    flip_weights(weight, starts, span_at * rows + first_row, first_column, flipped)
    inner = [first - start for first, start in zip(first_halo, columns)]
    weights = flipped[pl.ds(by_span(span_at, inner, 16), halo), :]
    number = table_ref.shape[2]
    for j in range(instances):
        fetched[j].wait()
        taken = planes_ref[:, edge_rows, :] if j == 0 else edges[j - 1]
        result = jnp.dot(
            taken.reshape(fields * edge, pitch),
            table_ref[j],
            preferred_element_type=jnp.float32,
        ).astype(jnp.bfloat16)
        for f in range(fields):
            at = (j * fields + f) * number
            spectra[:, at : at + number] = result[f * edge : (f + 1) * edge]
    result = jnp.dot(weights, spectra[...], preferred_element_type=jnp.float32)
    for j in range(instances):
        for f in range(fields):
            at = (j * fields + f) * number
            halo_refs[j][f] = result[:, at : at + number].astype(jnp.bfloat16)
    rest_fetched.wait()


def edge_call(sizes, counts, orders, starts, weight, planes):
    instances, fields, rs_loc, halo, edge, total_pitch = sizes
    pitch = planes.shape[2]
    columns = 2 * orders.shape[1]
    width = window((rs_loc, rs_loc - halo), halo)[1]
    count = instances * fields
    vmem = pl.BlockSpec(memory_space=pltpu.VMEM)
    hbm = pl.BlockSpec(memory_space=pltpu.HBM)
    return pl.pallas_call(
        functools.partial(edge_kernel, sizes),
        out_shape=[jax.ShapeDtypeStruct((fields, halo, columns), jnp.bfloat16)] * instances
        + [
            jax.ShapeDtypeStruct((instances, pitch, columns), jnp.bfloat16),
            pltpu.VMEM((fields, *planes.shape[1:]), jnp.bfloat16),
        ],
        in_specs=[hbm] * 5,
        out_specs=[vmem] * (instances + 2),
        scratch_shapes=[
            pltpu.SMEM(counts.shape, jnp.int32),
            pltpu.VMEM(orders.shape, jnp.int32),
            pltpu.VMEM(starts.shape, jnp.int32),
            pltpu.VMEM((edge, width), jnp.bfloat16),
            pltpu.VMEM((max(instances - 1, 1), fields, edge, pitch), jnp.bfloat16),
            pltpu.VMEM((width, edge), jnp.bfloat16),
            pltpu.VMEM((edge, count * columns), jnp.bfloat16),
            pltpu.SemaphoreType.DMA((4,)),
            pltpu.SemaphoreType.DMA((instances + 1,)),
        ],
        compiler_params=pltpu.CompilerParams(vmem_limit_bytes=VMEM_BYTES),
        cost_estimate=pl.CostEstimate(
            flops=2 * count * edge * columns * (pitch + halo),
            bytes_accessed=2 * count * edge * pitch,
            transcendentals=0,
        ),
        name="edge",
    )(counts, orders, starts, weight, planes)


def analyse_planes(planes_ref, table_ref, band_ref, spectra, out_refs):
    fields, rows, pitch = planes_ref.shape
    columns = table_ref.shape[1]
    per = band_ref.shape[0] // len(out_refs)
    result = jnp.dot(
        planes_ref[...].reshape(fields * rows, pitch),
        table_ref[...],
        preferred_element_type=jnp.float32,
    ).astype(jnp.bfloat16)
    for f in range(fields):
        spectra[:, f * columns : (f + 1) * columns] = result[f * rows : (f + 1) * rows]
    result = jnp.dot(band_ref[...], spectra[...], preferred_element_type=jnp.float32)
    for k, out_ref in enumerate(out_refs):
        for f in range(fields):
            out_ref[f] = result[
                k * per : (k + 1) * per, f * columns : (f + 1) * columns
            ].astype(out_ref.dtype)


def next_planes(planes_hbm, part, next_ref, sem):
    return pltpu.make_async_copy(
        planes_hbm.at[pl.ds((part + 1) * next_ref.shape[0], next_ref.shape[0])], next_ref, sem
    )


def first_kernel(
    sizes, shards, starts_hbm, weight_hbm, planes_hbm, planes_ref, table_ref, *rest,
):
    instances, fields, rs_loc, halo, edge, total_pitch = sizes
    out_refs, band_ref, next_refs = rest[:shards], rest[shards], rest[shards + 1 : -5]
    starts, weight, flipped, spectra, sems = rest[-5:]
    rows = weight_hbm.shape[0]
    per = rs_loc // shards
    span_at = lax.axis_index("span")
    pitch_at = lax.axis_index("pitch")
    columns, width = window((0, rs_loc), rs_loc)
    first_column = by_span(span_at, columns, LANES)
    small = started(
        pltpu.make_async_copy(starts_hbm, starts, sems.at[0]),
        pltpu.make_async_copy(weight_hbm.at[:, pl.ds(first_column, width)], weight, sems.at[1]),
    )
    following = started(*(next_planes(planes_hbm, 0, ref, sems.at[2]) for ref in next_refs))
    for copy in small:
        copy.wait()
    flip_weights(weight, starts, span_at * rows, first_column, flipped)
    own = by_span(span_at, (0, rs_loc - columns[1]), 16)
    for k in range(shards):
        at = jnp.bitwise_xor(pitch_at, k) if shards > 1 else 0
        source = pl.multiple_of(own + at * per, 16)
        band_ref[k * per : (k + 1) * per] = flipped[pl.ds(source, per), :]
    analyse_planes(planes_ref, table_ref.at[0], band_ref, spectra, out_refs)
    for copy in following:
        copy.wait()


def own_shapes(shards, fields, per, columns):
    kinds = [jnp.bfloat16 if k % 2 else jnp.float32 for k in range(shards)]
    return [jax.ShapeDtypeStruct((fields, per, columns), kind) for kind in kinds]


def first_call(sizes, shards, starts, weight, planes, held, table):
    instances, fields, rs_loc, halo, edge, total_pitch = sizes
    rows, pitch = planes.shape[1:]
    columns = table.shape[2]
    width = window((0, rs_loc), rs_loc)[1]
    vmem = pl.BlockSpec(memory_space=pltpu.VMEM)
    hbm = pl.BlockSpec(memory_space=pltpu.HBM)
    following = [pltpu.VMEM((fields, rows, pitch), jnp.bfloat16)] * (instances > 1)
    return pl.pallas_call(
        functools.partial(first_kernel, sizes, shards),
        out_shape=own_shapes(shards, fields, rs_loc // shards, columns)
        + [jax.ShapeDtypeStruct((rs_loc, rows), jnp.bfloat16)]
        + following,
        in_specs=[hbm, hbm, hbm, vmem, vmem],
        out_specs=[vmem] * (shards + 1 + len(following)),
        scratch_shapes=[
            pltpu.VMEM(starts.shape, jnp.int32),
            pltpu.VMEM((rows, width), jnp.bfloat16),
            pltpu.VMEM((width, rows), jnp.bfloat16),
            pltpu.VMEM((rows, fields * columns), jnp.bfloat16),
            pltpu.SemaphoreType.DMA((3,)),
        ],
        compiler_params=pltpu.CompilerParams(vmem_limit_bytes=VMEM_BYTES),
        cost_estimate=pl.CostEstimate(
            flops=2 * fields * rows * columns * (pitch + rs_loc),
            bytes_accessed=2 * fields * rows * pitch,
            transcendentals=0,
        ),
        name="first_part",
    )(starts, weight, planes, held, table)


def later_kernel(
    sizes, shards, part,
    counts_hbm, orders_hbm, planes_hbm, planes_ref, table_ref, band_ref, after_ref, *rest,
):
    out_refs, synthesis_ref, next_refs = rest[:shards], rest[shards], rest[shards + 1 : -4]
    counts, orders, spectra, sems = rest[-4:]
    small = started(
        pltpu.make_async_copy(counts_hbm, counts, sems.at[0]),
        pltpu.make_async_copy(orders_hbm, orders, sems.at[1]),
    )
    following = started(*(next_planes(planes_hbm, part, ref, sems.at[2]) for ref in next_refs))
    analyse_planes(planes_ref, table_ref.at[part], band_ref, spectra, out_refs)
    for copy in small:
        copy.wait()
    wave = column_wavenumbers(counts, orders)
    pitch = synthesis_ref.shape[0]
    factors = table_factors(wave, lax.axis_index("pitch") * pitch, pitch, sizes[-1], 0.0)
    fill_table(synthesis_ref, (), factors, 1.0 / math.sqrt(wave.shape[1] // 2))
    for copy in following:
        copy.wait()


def later_call(sizes, shards, part, counts, orders, planes, held, table, band, after):
    instances, fields, rs_loc, halo, edge, total_pitch = sizes
    rows, pitch = planes.shape[1:]
    columns = table.shape[2]
    vmem = pl.BlockSpec(memory_space=pltpu.VMEM)
    hbm = pl.BlockSpec(memory_space=pltpu.HBM)
    following = [pltpu.VMEM((fields, rows, pitch), jnp.bfloat16)] * (part + 1 < instances)
    return pl.pallas_call(
        functools.partial(later_kernel, sizes, shards, part),
        out_shape=own_shapes(shards, fields, rs_loc // shards, columns)
        + [jax.ShapeDtypeStruct((pitch, columns), jnp.bfloat16)]
        + following,
        in_specs=[hbm, hbm, hbm, vmem, vmem, vmem, pl.BlockSpec(memory_space=pl.ANY)],
        out_specs=[vmem] * (shards + 1 + len(following)),
        scratch_shapes=[
            pltpu.SMEM(counts.shape, jnp.int32),
            pltpu.VMEM(orders.shape, jnp.int32),
            pltpu.VMEM((rows, fields * columns), jnp.bfloat16),
            pltpu.SemaphoreType.DMA((3,)),
        ],
        compiler_params=pltpu.CompilerParams(vmem_limit_bytes=VMEM_BYTES),
        cost_estimate=pl.CostEstimate(
            flops=2 * fields * rows * columns * (pitch + rs_loc),
            bytes_accessed=2 * fields * rows * pitch,
            transcendentals=0,
        ),
        name="later_part",
    )(counts, orders, planes, held, table, band, after)


def synthesise_kernel(fields, ranks, shards, per, table_ref, *rest):
    piece_refs = rest[: len(ranks)]
    out_hbm, rows_ref, sems = rest[-3:]
    pitch_at = lax.axis_index("pitch")
    copies = []
    for i, (part, k) in enumerate(ranks):
        piece = piece_refs[i][...]
        value = lax.dot_general(
            piece.reshape(fields * per, piece.shape[2]),
            table_ref[...],
            (((1,), (1,)), ((), ())),
            preferred_element_type=jnp.float32,
        )
        rows_ref[i] = value.astype(rows_ref.dtype).reshape(fields, per, value.shape[1])
        at = jnp.bitwise_xor(pitch_at, k) if shards > 1 else 0
        copies += started(
            pltpu.make_async_copy(
                rows_ref.at[i],
                out_hbm.at[
                    pl.ds(part * fields, fields), pl.ds(pl.multiple_of(at * per, 16), per), :
                ],
                sems.at[i],
            )
        )
    for copy in copies:
        copy.wait()


def synthesise_call(count, shards, table, pieces, base):
    ranks = list(pieces)
    fields, per, columns = pieces[ranks[0]].shape
    pitch = table.shape[0]
    vmem = pl.BlockSpec(memory_space=pltpu.VMEM)
    hbm = pl.BlockSpec(memory_space=pltpu.HBM)
    operands = [table, *pieces.values()]
    in_specs = [vmem] * len(operands)
    aliases = {}
    if base is not None:
        aliases = {len(operands): 0}
        operands.append(base)
        in_specs.append(hbm)
    return pl.pallas_call(
        functools.partial(synthesise_kernel, fields, ranks, shards, per),
        out_shape=jax.ShapeDtypeStruct((count, per * shards, pitch), jnp.bfloat16),
        in_specs=in_specs,
        out_specs=hbm,
        scratch_shapes=[
            pltpu.VMEM((len(ranks), fields, per, pitch), jnp.bfloat16),
            pltpu.SemaphoreType.DMA((len(ranks),)),
        ],
        input_output_aliases=aliases,
        compiler_params=pltpu.CompilerParams(vmem_limit_bytes=VMEM_BYTES),
        cost_estimate=pl.CostEstimate(
            flops=2 * len(ranks) * fields * per * columns * pitch,
            bytes_accessed=2 * len(ranks) * fields * per * pitch,
            transcendentals=0,
        ),
        name="synthesise",
    )(*operands)


def body(outlet, remap_weight, band_start, blade_counts, mode_orders):
    row_count = lax.axis_size("row")
    pitch_count = lax.axis_size("pitch")
    instances, fields, rows, pitch = outlet.shape[1:]
    stator_rows = remap_weight.shape[1]
    total_pitch = pitch * pitch_count
    rs_loc, halo_rows, edge = geometry(outlet.shape, stator_rows)
    count = instances * fields
    by_shards = (
        pitch_count == 4
        and rs_loc % (16 * pitch_count) == 0
        and halo_rows == rs_loc // pitch_count
    )
    shards = pitch_count if by_shards else 1
    shift = row_count // 2

    def stay(value):
        return pltpu.with_memory_space_constraint(value, pltpu.HBM)

    planes = stay(outlet.reshape(count, rows, pitch))
    orders = stay(mode_orders.T)
    starts = stay(band_start.reshape(stator_rows // LANES, LANES))
    blade_counts = stay(blade_counts)
    remap_weight = stay(remap_weight)
    sizes = (instances, fields, rs_loc, halo_rows, edge, total_pitch)
    halo_at = jnp.where(lax.axis_index("span") == 0, shards - 1, 0)
    holds = [jnp.bitwise_xor(lax.axis_index("pitch"), k) == halo_at for k in range(shards)]
    *halos, table, held = edge_call(
        sizes, after(blade_counts, *holds), orders, starts, remap_weight, planes
    )
    made = first_call(sizes, shards, starts, remap_weight, planes, held, table)
    owns, band, held = [made[:shards]], made[shards], made[-1]
    known = {}

    def get(kind, part):
        if (kind, part) not in known:
            known[kind, part] = steps[kind](part)
        return known[kind, part]

    def ready(kind, part, value):
        return after(value, *(get(*step) for step in ORDER.get((kind, part), ())))

    def later(part):
        if part == 0:
            return owns[0][-1]
        first_sent = halos[0] if shards == 1 else get("meet", 0)[1]
        made = later_call(
            sizes, shards, part, blade_counts, orders, planes,
            known.get(("held", part), held), table, band, ready("later", part, first_sent),
        )
        owns.append(made[:shards])
        known["synthesis", 0] = made[shards]
        known["held", part + 1] = made[-1]
        return made[0]

    def halo(part):
        return exchange(ready("halo", part, halos[part]), "span", 1)

    def with_halo(part, k, *terms):
        get("later", part)
        total = jnp.where(holds[k], get("halo", part).astype(jnp.float32), 0.0)
        for term in (owns[part][k], *terms):
            total = total + term.astype(jnp.float32)
        return total.astype(jnp.bfloat16)

    def meet(part):
        return None, with_halo(part, 3)

    def pair_sent(part):
        sent = [get("meet", part)[1]]
        if part > 0 and JOIN:
            sent.append(with_halo(part - 1, 1))
        return exchange(ready("pair", part, jnp.stack(sent)), "pitch", 1)

    def pair(part):
        return get("pair_sent", part)[0]

    def beside(part):
        if part + 1 < instances and JOIN:
            return get("pair_sent", part + 1)[1]
        return exchange(ready("beside", part, with_halo(part, 1)), "pitch", 1)

    def across(part):
        return exchange(
            ready("across", part, with_halo(part, 2, get("pair", part))), "pitch", 2
        )

    def total(part):
        return with_halo(part, 0, get("beside", part), get("across", part))

    def spread(value, k):
        pairs = [
            (g * pitch_count + z, ((g + shift) % row_count) * pitch_count + (z ^ k))
            for g in range(row_count)
            for z in range(pitch_count)
        ]
        return lax.ppermute(value, ("row", "pitch"), pairs)

    def swap(part):
        return spread(ready("swap", part, get("total", part)), 0)

    def swap_across(part):
        return spread(ready("swap_across", part, get("total", part)), 2)

    def swap_beside(part):
        if DIRECT:
            return spread(ready("swap_beside", part, get("total", part)), 1)
        return exchange(ready("swap_beside", part, get("swap", part)), "pitch", 1)

    def across_on(part):
        return exchange(ready("across_on", part, get("swap_across", part)), "pitch", 1)

    def synth(at):
        base = get("synth", at - 1) if at else None
        group = {(part, k): get(names[k], part) for part, k in GROUPS[at]}
        return synthesise_call(count, shards, known["synthesis", 0], group, base)

    steps = dict(
        synth=synth,
        later=later, halo=halo, meet=meet, pair_sent=pair_sent, pair=pair, beside=beside, across=across, total=total,
        swap=swap, swap_across=swap_across, swap_beside=swap_beside, across_on=across_on,
    )
    names = ("swap", "swap_beside", "swap_across", "across_on")

    def whole_sum(part):
        get("later", part)
        wide = get("halo", part).astype(jnp.float32)
        low = jnp.pad(wide, ((0, 0), (rs_loc - halo_rows, 0), (0, 0)))
        high = jnp.pad(wide, ((0, 0), (0, rs_loc - halo_rows), (0, 0)))
        mine = owns[part][0] + jnp.where(lax.axis_index("span") == 0, low, high)
        return lax.psum(mine, "pitch").astype(jnp.bfloat16)

    joined = None
    get("later", instances - 1)
    if by_shards:
        joined = get("synth", len(GROUPS) - 1)
    else:
        pairs = [(g, (g + shift) % row_count) for g in range(row_count)]
        pieces = {
            (part, 0): lax.ppermute(whole_sum(part), "row", pairs) for part in range(instances)
        }
        joined = synthesise_call(count, shards, known["synthesis", 0], pieces, joined)
    return joined.reshape(1, instances, fields, rs_loc, pitch)


def solution(mesh):
    placed = (P("row", None, None, "span", "pitch"), P("span", None), P(), P(), P())
    return jax.shard_map(
        body,
        mesh=mesh,
        in_specs=placed,
        out_specs=P("row", None, None, "span", "pitch"),
        check_vma=False,
    )
```

```python
import functools
import math

import jax
import jax.numpy as jnp
from jax import lax
from jax.experimental import pallas as pl
from jax.experimental.pallas import tpu as pltpu
from jax.sharding import PartitionSpec as P

BAND = 192
JITTER = 6
LANES = 128
ORDER = {('halo', 1): (('halo', 0),)}
JOIN = 0
DIRECT = (0, 1)
GROUPS = (((0, 0), (0, 1), (0, 2), (0, 3), (1, 0), (1, 2)), ((1, 1), (1, 3)))
VMEM_BYTES = 32 * 1024 * 1024


def exchange(value, axis, distance):
    count = lax.axis_size(axis)
    return lax.ppermute(value, axis, [(i, i ^ distance) for i in range(count)])


def after(value, *others):
    return lax.optimization_barrier((value, *others))[0] if others else value


def column_wavenumbers(counts_ref, orders_ref):
    harmonics = orders_ref.shape[1]
    columns = 2 * harmonics
    spread = (
        lax.broadcasted_iota(jnp.int32, (harmonics, columns), 1) // 2
        == lax.broadcasted_iota(jnp.int32, (harmonics, columns), 0)
    )
    orders = jnp.dot(
        orders_ref[...].astype(jnp.float32),
        spread.astype(jnp.float32),
        preferred_element_type=jnp.float32,
    ).astype(jnp.int32)
    return orders[0:1] * counts_ref[0] + orders[1:2] * counts_ref[1]


def table_factors(wave, first_row, rows, total_pitch, turn):
    fine = 32
    coarse = rows // fine
    columns = wave.shape[1]
    step = 2.0 * math.pi / total_pitch
    at_coarse = first_row + fine * lax.broadcasted_iota(jnp.int32, (coarse, columns), 0)
    at_fine = lax.broadcasted_iota(jnp.int32, (fine, columns), 0)
    odd = lax.broadcasted_iota(jnp.int32, (fine, columns), 1) % 2
    q_coarse = lax.rem(at_coarse * wave, total_pitch)
    q_fine = lax.rem(at_fine * wave - odd * (total_pitch // 4), total_pitch)
    a = step * q_coarse.astype(jnp.float32)
    b = step * q_fine.astype(jnp.float32) + turn
    return jnp.cos(a), jnp.sin(a), jnp.cos(b), jnp.sin(b)


def fill_table(ref, at, factors, scale):
    cos_a, sin_a, cos_b, sin_b = factors
    fine = cos_b.shape[0]
    cos_b = cos_b * scale
    sin_b = sin_b * scale
    for i in range(cos_a.shape[0]):
        value = cos_a[i : i + 1] * cos_b - sin_a[i : i + 1] * sin_b
        ref[at + (pl.ds(i * fine, fine), slice(None))] = value.astype(ref.dtype)


def geometry(outlet_shape, stator_rows):
    rows = outlet_shape[-2]
    total_rows = 2 * rows
    rs_loc = stator_rows // 2
    slope = (stator_rows - 1) / (total_rows - BAND)
    above = math.floor((rows - 1 + JITTER) * slope) + 1 - rs_loc
    below = rs_loc - math.ceil((rows - BAND + 1 - JITTER) * slope)
    halo = -(-max(above, below) // 16) * 16
    reach = max(
        rows - math.floor(rs_loc / slope - JITTER),
        math.floor((rs_loc - 1) / slope + JITTER) + BAND - rows,
    )
    edge = -(-reach // LANES) * LANES
    return rs_loc, halo, edge


def window(first, number):
    starts = [at // LANES * LANES for at in first]
    width = max(-(-(at + number) // LANES) * LANES - start for at, start in zip(first, starts))
    return starts, width


def by_span(span_at, values, multiple):
    return pl.multiple_of(jnp.where(span_at == 0, values[0], values[1]), multiple)


def flip_weights(weight_ref, starts_ref, first_row, first_column, flipped):
    rows, width = weight_ref.shape
    row = first_row + lax.broadcasted_iota(jnp.int32, (rows, LANES), 0)
    for block in range(width // LANES):
        start = starts_ref[pl.ds(first_column // LANES + block, 1), :]
        inside = (row >= start) & (row < start + BAND)
        at = slice(block * LANES, (block + 1) * LANES)
        value = jnp.where(inside, weight_ref[:, at].astype(jnp.float32), 0.0)
        flipped[at, :] = value.T.astype(flipped.dtype)


def instance_turn(wave, instance, period):
    whole = period.astype(jnp.float32)
    steps = (wave * instance).astype(jnp.float32)
    return (2.0 * math.pi) * (steps - whole * jnp.floor(steps / whole)) / whole


def fill_analysis(wave, counts_ref, part, instances, total_pitch, table_ref):
    pitch = table_ref.shape[0]
    instance = lax.axis_index("row") * instances + part
    period = lax.axis_size("row") * instances * counts_ref[0]
    turn = instance_turn(wave, instance, period)
    factors = table_factors(wave, lax.axis_index("pitch") * pitch, pitch, total_pitch, turn)
    fill_table(table_ref, (), factors, math.sqrt(2.0 / total_pitch))


def started(*copies):
    for copy in copies:
        copy.start()
    return copies


def edge_kernel(
    sizes, counts_hbm, orders_hbm, starts_hbm, weight_hbm, planes_hbm, *rest,
):
    instances, fields, rs_loc, halo, edge, total_pitch = sizes
    halo_refs, (table_ref, planes_ref) = rest[:instances], rest[instances : instances + 2]
    counts, orders, starts, weight, edges, flipped, spectra, sems, plane_sems = rest[
        instances + 2 :
    ]
    rows, pitch = planes_hbm.shape[1:]
    others = rows - edge
    span_at = lax.axis_index("span")
    first_halo = (rs_loc, rs_loc - halo)
    columns, width = window(first_halo, halo)
    first_row = pl.multiple_of((1 - span_at) * (rows - edge), 16)
    first_column = by_span(span_at, columns, LANES)
    small = started(
        pltpu.make_async_copy(counts_hbm, counts, sems.at[0]),
        pltpu.make_async_copy(orders_hbm, orders, sems.at[1]),
        pltpu.make_async_copy(starts_hbm, starts, sems.at[2]),
        pltpu.make_async_copy(
            weight_hbm.at[pl.ds(first_row, edge), pl.ds(first_column, width)], weight, sems.at[3]
        ),
    )
    edge_rows = pl.ds(first_row, edge)
    other_rows = pl.ds(pl.multiple_of(span_at * edge, 16), others)
    fetched = started(
        pltpu.make_async_copy(
            planes_hbm.at[pl.ds(0, fields), edge_rows, :],
            planes_ref.at[:, edge_rows, :],
            plane_sems.at[0],
        ),
        *(
            pltpu.make_async_copy(
                planes_hbm.at[pl.ds(j * fields, fields), edge_rows, :],
                edges.at[j - 1],
                plane_sems.at[j],
            )
            for j in range(1, instances)
        ),
    )
    (rest_fetched,) = started(
        pltpu.make_async_copy(
            planes_hbm.at[pl.ds(0, fields), other_rows, :],
            planes_ref.at[:, other_rows, :],
            plane_sems.at[instances],
        )
    )
    for copy in small[:2]:
        copy.wait()
    wave = column_wavenumbers(counts, orders)
    for j in range(instances):
        fill_analysis(wave, counts, j, instances, total_pitch, table_ref.at[j])
    for copy in small[2:]:
        copy.wait()
    flip_weights(weight, starts, span_at * rows + first_row, first_column, flipped)
    inner = [first - start for first, start in zip(first_halo, columns)]
    weights = flipped[pl.ds(by_span(span_at, inner, 16), halo), :]
    number = table_ref.shape[2]
    for j in range(instances):
        fetched[j].wait()
        taken = planes_ref[:, edge_rows, :] if j == 0 else edges[j - 1]
        result = jnp.dot(
            taken.reshape(fields * edge, pitch),
            table_ref[j],
            preferred_element_type=jnp.float32,
        ).astype(jnp.bfloat16)
        for f in range(fields):
            at = (j * fields + f) * number
            spectra[:, at : at + number] = result[f * edge : (f + 1) * edge]
    result = jnp.dot(weights, spectra[...], preferred_element_type=jnp.float32)
    for j in range(instances):
        for f in range(fields):
            at = (j * fields + f) * number
            halo_refs[j][f] = result[:, at : at + number].astype(jnp.bfloat16)
    rest_fetched.wait()


def edge_call(sizes, counts, orders, starts, weight, planes):
    instances, fields, rs_loc, halo, edge, total_pitch = sizes
    pitch = planes.shape[2]
    columns = 2 * orders.shape[1]
    width = window((rs_loc, rs_loc - halo), halo)[1]
    count = instances * fields
    vmem = pl.BlockSpec(memory_space=pltpu.VMEM)
    hbm = pl.BlockSpec(memory_space=pltpu.HBM)
    return pl.pallas_call(
        functools.partial(edge_kernel, sizes),
        out_shape=[jax.ShapeDtypeStruct((fields, halo, columns), jnp.bfloat16)] * instances
        + [
            jax.ShapeDtypeStruct((instances, pitch, columns), jnp.bfloat16),
            pltpu.VMEM((fields, *planes.shape[1:]), jnp.bfloat16),
        ],
        in_specs=[hbm] * 5,
        out_specs=[vmem] * (instances + 2),
        scratch_shapes=[
            pltpu.SMEM(counts.shape, jnp.int32),
            pltpu.VMEM(orders.shape, jnp.int32),
            pltpu.VMEM(starts.shape, jnp.int32),
            pltpu.VMEM((edge, width), jnp.bfloat16),
            pltpu.VMEM((max(instances - 1, 1), fields, edge, pitch), jnp.bfloat16),
            pltpu.VMEM((width, edge), jnp.bfloat16),
            pltpu.VMEM((edge, count * columns), jnp.bfloat16),
            pltpu.SemaphoreType.DMA((4,)),
            pltpu.SemaphoreType.DMA((instances + 1,)),
        ],
        compiler_params=pltpu.CompilerParams(vmem_limit_bytes=VMEM_BYTES),
        cost_estimate=pl.CostEstimate(
            flops=2 * count * edge * columns * (pitch + halo),
            bytes_accessed=2 * count * edge * pitch,
            transcendentals=0,
        ),
        name="edge",
    )(counts, orders, starts, weight, planes)


def analyse_planes(planes_ref, table_ref, band_ref, spectra, out_refs):
    fields, rows, pitch = planes_ref.shape
    columns = table_ref.shape[1]
    per = band_ref.shape[0] // len(out_refs)
    result = jnp.dot(
        planes_ref[...].reshape(fields * rows, pitch),
        table_ref[...],
        preferred_element_type=jnp.float32,
    ).astype(jnp.bfloat16)
    for f in range(fields):
        spectra[:, f * columns : (f + 1) * columns] = result[f * rows : (f + 1) * rows]
    result = jnp.dot(band_ref[...], spectra[...], preferred_element_type=jnp.float32)
    for k, out_ref in enumerate(out_refs):
        for f in range(fields):
            out_ref[f] = result[
                k * per : (k + 1) * per, f * columns : (f + 1) * columns
            ].astype(out_ref.dtype)


def next_planes(planes_hbm, part, next_ref, sem):
    return pltpu.make_async_copy(
        planes_hbm.at[pl.ds((part + 1) * next_ref.shape[0], next_ref.shape[0])], next_ref, sem
    )


def first_kernel(
    sizes, shards, starts_hbm, weight_hbm, planes_hbm, planes_ref, table_ref, *rest,
):
    instances, fields, rs_loc, halo, edge, total_pitch = sizes
    out_refs, band_ref, next_refs = rest[:shards], rest[shards], rest[shards + 1 : -5]
    starts, weight, flipped, spectra, sems = rest[-5:]
    rows = weight_hbm.shape[0]
    per = rs_loc // shards
    span_at = lax.axis_index("span")
    pitch_at = lax.axis_index("pitch")
    columns, width = window((0, rs_loc), rs_loc)
    first_column = by_span(span_at, columns, LANES)
    small = started(
        pltpu.make_async_copy(starts_hbm, starts, sems.at[0]),
        pltpu.make_async_copy(weight_hbm.at[:, pl.ds(first_column, width)], weight, sems.at[1]),
    )
    following = started(*(next_planes(planes_hbm, 0, ref, sems.at[2]) for ref in next_refs))
    for copy in small:
        copy.wait()
    flip_weights(weight, starts, span_at * rows, first_column, flipped)
    own = by_span(span_at, (0, rs_loc - columns[1]), 16)
    for k in range(shards):
        at = jnp.bitwise_xor(pitch_at, k) if shards > 1 else 0
        source = pl.multiple_of(own + at * per, 16)
        band_ref[k * per : (k + 1) * per] = flipped[pl.ds(source, per), :]
    analyse_planes(planes_ref, table_ref.at[0], band_ref, spectra, out_refs)
    for copy in following:
        copy.wait()


def own_shapes(shards, fields, per, columns):
    kinds = [jnp.bfloat16 if k % 2 else jnp.float32 for k in range(shards)]
    return [jax.ShapeDtypeStruct((fields, per, columns), kind) for kind in kinds]


def first_call(sizes, shards, starts, weight, planes, held, table):
    instances, fields, rs_loc, halo, edge, total_pitch = sizes
    rows, pitch = planes.shape[1:]
    columns = table.shape[2]
    width = window((0, rs_loc), rs_loc)[1]
    vmem = pl.BlockSpec(memory_space=pltpu.VMEM)
    hbm = pl.BlockSpec(memory_space=pltpu.HBM)
    following = [pltpu.VMEM((fields, rows, pitch), jnp.bfloat16)] * (instances > 1)
    return pl.pallas_call(
        functools.partial(first_kernel, sizes, shards),
        out_shape=own_shapes(shards, fields, rs_loc // shards, columns)
        + [jax.ShapeDtypeStruct((rs_loc, rows), jnp.bfloat16)]
        + following,
        in_specs=[hbm, hbm, hbm, vmem, vmem],
        out_specs=[vmem] * (shards + 1 + len(following)),
        scratch_shapes=[
            pltpu.VMEM(starts.shape, jnp.int32),
            pltpu.VMEM((rows, width), jnp.bfloat16),
            pltpu.VMEM((width, rows), jnp.bfloat16),
            pltpu.VMEM((rows, fields * columns), jnp.bfloat16),
            pltpu.SemaphoreType.DMA((3,)),
        ],
        compiler_params=pltpu.CompilerParams(vmem_limit_bytes=VMEM_BYTES),
        cost_estimate=pl.CostEstimate(
            flops=2 * fields * rows * columns * (pitch + rs_loc),
            bytes_accessed=2 * fields * rows * pitch,
            transcendentals=0,
        ),
        name="first_part",
    )(starts, weight, planes, held, table)


def later_kernel(
    sizes, shards, part,
    counts_hbm, orders_hbm, planes_hbm, planes_ref, table_ref, band_ref, after_ref, *rest,
):
    out_refs, synthesis_ref, next_refs = rest[:shards], rest[shards], rest[shards + 1 : -4]
    counts, orders, spectra, sems = rest[-4:]
    small = started(
        pltpu.make_async_copy(counts_hbm, counts, sems.at[0]),
        pltpu.make_async_copy(orders_hbm, orders, sems.at[1]),
    )
    following = started(*(next_planes(planes_hbm, part, ref, sems.at[2]) for ref in next_refs))
    analyse_planes(planes_ref, table_ref.at[part], band_ref, spectra, out_refs)
    for copy in small:
        copy.wait()
    wave = column_wavenumbers(counts, orders)
    pitch = synthesis_ref.shape[0]
    factors = table_factors(wave, lax.axis_index("pitch") * pitch, pitch, sizes[-1], 0.0)
    fill_table(synthesis_ref, (), factors, 1.0 / math.sqrt(wave.shape[1] // 2))
    for copy in following:
        copy.wait()


def later_call(sizes, shards, part, counts, orders, planes, held, table, band, after):
    instances, fields, rs_loc, halo, edge, total_pitch = sizes
    rows, pitch = planes.shape[1:]
    columns = table.shape[2]
    vmem = pl.BlockSpec(memory_space=pltpu.VMEM)
    hbm = pl.BlockSpec(memory_space=pltpu.HBM)
    following = [pltpu.VMEM((fields, rows, pitch), jnp.bfloat16)] * (part + 1 < instances)
    return pl.pallas_call(
        functools.partial(later_kernel, sizes, shards, part),
        out_shape=own_shapes(shards, fields, rs_loc // shards, columns)
        + [jax.ShapeDtypeStruct((pitch, columns), jnp.bfloat16)]
        + following,
        in_specs=[hbm, hbm, hbm, vmem, vmem, vmem, pl.BlockSpec(memory_space=pl.ANY)],
        out_specs=[vmem] * (shards + 1 + len(following)),
        scratch_shapes=[
            pltpu.SMEM(counts.shape, jnp.int32),
            pltpu.VMEM(orders.shape, jnp.int32),
            pltpu.VMEM((rows, fields * columns), jnp.bfloat16),
            pltpu.SemaphoreType.DMA((3,)),
        ],
        compiler_params=pltpu.CompilerParams(vmem_limit_bytes=VMEM_BYTES),
        cost_estimate=pl.CostEstimate(
            flops=2 * fields * rows * columns * (pitch + rs_loc),
            bytes_accessed=2 * fields * rows * pitch,
            transcendentals=0,
        ),
        name="later_part",
    )(counts, orders, planes, held, table, band, after)


def synthesise_kernel(fields, ranks, shards, per, table_ref, *rest):
    piece_refs = rest[: len(ranks)]
    out_hbm, rows_ref, sems = rest[-3:]
    pitch_at = lax.axis_index("pitch")
    copies = []
    for i, (part, k) in enumerate(ranks):
        piece = piece_refs[i][...]
        value = lax.dot_general(
            piece.reshape(fields * per, piece.shape[2]),
            table_ref[...],
            (((1,), (1,)), ((), ())),
            preferred_element_type=jnp.float32,
        )
        rows_ref[i] = value.astype(rows_ref.dtype).reshape(fields, per, value.shape[1])
        at = jnp.bitwise_xor(pitch_at, k) if shards > 1 else 0
        copies += started(
            pltpu.make_async_copy(
                rows_ref.at[i],
                out_hbm.at[
                    pl.ds(part * fields, fields), pl.ds(pl.multiple_of(at * per, 16), per), :
                ],
                sems.at[i],
            )
        )
    for copy in copies:
        copy.wait()


def synthesise_call(count, shards, table, pieces, base):
    ranks = list(pieces)
    fields, per, columns = pieces[ranks[0]].shape
    pitch = table.shape[0]
    vmem = pl.BlockSpec(memory_space=pltpu.VMEM)
    hbm = pl.BlockSpec(memory_space=pltpu.HBM)
    operands = [table, *pieces.values()]
    in_specs = [vmem] * len(operands)
    aliases = {}
    if base is not None:
        aliases = {len(operands): 0}
        operands.append(base)
        in_specs.append(hbm)
    return pl.pallas_call(
        functools.partial(synthesise_kernel, fields, ranks, shards, per),
        out_shape=jax.ShapeDtypeStruct((count, per * shards, pitch), jnp.bfloat16),
        in_specs=in_specs,
        out_specs=hbm,
        scratch_shapes=[
            pltpu.VMEM((len(ranks), fields, per, pitch), jnp.bfloat16),
            pltpu.SemaphoreType.DMA((len(ranks),)),
        ],
        input_output_aliases=aliases,
        compiler_params=pltpu.CompilerParams(vmem_limit_bytes=VMEM_BYTES),
        cost_estimate=pl.CostEstimate(
            flops=2 * len(ranks) * fields * per * columns * pitch,
            bytes_accessed=2 * len(ranks) * fields * per * pitch,
            transcendentals=0,
        ),
        name="synthesise",
    )(*operands)


def body(outlet, remap_weight, band_start, blade_counts, mode_orders):
    row_count = lax.axis_size("row")
    pitch_count = lax.axis_size("pitch")
    instances, fields, rows, pitch = outlet.shape[1:]
    stator_rows = remap_weight.shape[1]
    total_pitch = pitch * pitch_count
    rs_loc, halo_rows, edge = geometry(outlet.shape, stator_rows)
    count = instances * fields
    by_shards = (
        pitch_count == 4
        and rs_loc % (16 * pitch_count) == 0
        and halo_rows == rs_loc // pitch_count
    )
    shards = pitch_count if by_shards else 1
    shift = row_count // 2

    def stay(value):
        return pltpu.with_memory_space_constraint(value, pltpu.HBM)

    planes = stay(outlet.reshape(count, rows, pitch))
    orders = stay(mode_orders.T)
    starts = stay(band_start.reshape(stator_rows // LANES, LANES))
    blade_counts = stay(blade_counts)
    remap_weight = stay(remap_weight)
    sizes = (instances, fields, rs_loc, halo_rows, edge, total_pitch)
    halo_at = jnp.where(lax.axis_index("span") == 0, shards - 1, 0)
    holds = [jnp.bitwise_xor(lax.axis_index("pitch"), k) == halo_at for k in range(shards)]
    *halos, table, held = edge_call(
        sizes, after(blade_counts, *holds), orders, starts, remap_weight, planes
    )
    made = first_call(sizes, shards, starts, remap_weight, planes, held, table)
    owns, band, held = [made[:shards]], made[shards], made[-1]
    known = {}

    def get(kind, part):
        if (kind, part) not in known:
            known[kind, part] = steps[kind](part)
        return known[kind, part]

    def ready(kind, part, value):
        return after(value, *(get(*step) for step in ORDER.get((kind, part), ())))

    def later(part):
        if part == 0:
            return owns[0][-1]
        first_sent = halos[0] if shards == 1 else get("meet", 0)[1]
        made = later_call(
            sizes, shards, part, blade_counts, orders, planes,
            known.get(("held", part), held), table, band, ready("later", part, first_sent),
        )
        owns.append(made[:shards])
        known["synthesis", 0] = made[shards]
        known["held", part + 1] = made[-1]
        return made[0]

    def halo(part):
        return exchange(ready("halo", part, halos[part]), "span", 1)

    def with_halo(part, k, *terms):
        get("later", part)
        total = jnp.where(holds[k], get("halo", part).astype(jnp.float32), 0.0)
        for term in (owns[part][k], *terms):
            total = total + term.astype(jnp.float32)
        return total.astype(jnp.bfloat16)

    def meet(part):
        return None, with_halo(part, 3)

    def pair_sent(part):
        sent = [get("meet", part)[1]]
        if JOIN == 2:
            sent.append(with_halo(part, 1))
        elif part > 0 and JOIN:
            sent.append(with_halo(part - 1, 1))
        return exchange(ready("pair", part, jnp.stack(sent)), "pitch", 1)

    def pair(part):
        return get("pair_sent", part)[0]

    def beside(part):
        if JOIN == 2:
            return get("pair_sent", part)[1]
        if part + 1 < instances and JOIN:
            return get("pair_sent", part + 1)[1]
        return exchange(ready("beside", part, with_halo(part, 1)), "pitch", 1)

    def across(part):
        return exchange(
            ready("across", part, with_halo(part, 2, get("pair", part))), "pitch", 2
        )

    def total(part):
        return with_halo(part, 0, get("beside", part), get("across", part))

    def spread(value, k):
        pairs = [
            (g * pitch_count + z, ((g + shift) % row_count) * pitch_count + (z ^ k))
            for g in range(row_count)
            for z in range(pitch_count)
        ]
        return lax.ppermute(value, ("row", "pitch"), pairs)

    def swap(part):
        return spread(ready("swap", part, get("total", part)), 0)

    def swap_across(part):
        return spread(ready("swap_across", part, get("total", part)), 2)

    def swap_beside(part):
        if part in DIRECT:
            return spread(ready("swap_beside", part, get("total", part)), 1)
        return exchange(ready("swap_beside", part, get("swap", part)), "pitch", 1)

    def across_on(part):
        return exchange(ready("across_on", part, get("swap_across", part)), "pitch", 1)

    def synth(at):
        base = get("synth", at - 1) if at else None
        group = {(part, k): get(names[k], part) for part, k in GROUPS[at]}
        return synthesise_call(count, shards, known["synthesis", 0], group, base)

    steps = dict(
        synth=synth,
        later=later, halo=halo, meet=meet, pair_sent=pair_sent, pair=pair, beside=beside, across=across, total=total,
        swap=swap, swap_across=swap_across, swap_beside=swap_beside, across_on=across_on,
    )
    names = ("swap", "swap_beside", "swap_across", "across_on")

    def whole_sum(part):
        get("later", part)
        wide = get("halo", part).astype(jnp.float32)
        low = jnp.pad(wide, ((0, 0), (rs_loc - halo_rows, 0), (0, 0)))
        high = jnp.pad(wide, ((0, 0), (0, rs_loc - halo_rows), (0, 0)))
        mine = owns[part][0] + jnp.where(lax.axis_index("span") == 0, low, high)
        return lax.psum(mine, "pitch").astype(jnp.bfloat16)

    joined = None
    get("later", instances - 1)
    if by_shards:
        joined = get("synth", len(GROUPS) - 1)
    else:
        pairs = [(g, (g + shift) % row_count) for g in range(row_count)]
        pieces = {
            (part, 0): lax.ppermute(whole_sum(part), "row", pairs) for part in range(instances)
        }
        joined = synthesise_call(count, shards, known["synthesis", 0], pieces, joined)
    return joined.reshape(1, instances, fields, rs_loc, pitch)


def solution(mesh):
    placed = (P("row", None, None, "span", "pitch"), P("span", None), P(), P(), P())
    return jax.shard_map(
        body,
        mesh=mesh,
        in_specs=placed,
        out_specs=P("row", None, None, "span", "pitch"),
        check_vma=False,
    )
```

```python
import functools
import math

import jax
import jax.numpy as jnp
from jax import lax
from jax.experimental import pallas as pl
from jax.experimental.pallas import tpu as pltpu
from jax.sharding import PartitionSpec as P

BAND = 192
JITTER = 6
LANES = 128
ORDER = {}
JOIN = 0
DIRECT = (1,)
GROUPS = (((0, 0), (0, 3)), ((1, 0), (1, 3), (0, 1), (0, 2)), ((1, 1), (1, 2)))
VMEM_BYTES = 32 * 1024 * 1024


def exchange(value, axis, distance):
    count = lax.axis_size(axis)
    return lax.ppermute(value, axis, [(i, i ^ distance) for i in range(count)])


def after(value, *others):
    return lax.optimization_barrier((value, *others))[0] if others else value


def column_wavenumbers(counts_ref, orders_ref):
    harmonics = orders_ref.shape[1]
    columns = 2 * harmonics
    spread = (
        lax.broadcasted_iota(jnp.int32, (harmonics, columns), 1) // 2
        == lax.broadcasted_iota(jnp.int32, (harmonics, columns), 0)
    )
    orders = jnp.dot(
        orders_ref[...].astype(jnp.float32),
        spread.astype(jnp.float32),
        preferred_element_type=jnp.float32,
    ).astype(jnp.int32)
    return orders[0:1] * counts_ref[0] + orders[1:2] * counts_ref[1]


def table_factors(wave, first_row, rows, total_pitch, turn):
    fine = 32
    coarse = rows // fine
    columns = wave.shape[1]
    step = 2.0 * math.pi / total_pitch
    at_coarse = first_row + fine * lax.broadcasted_iota(jnp.int32, (coarse, columns), 0)
    at_fine = lax.broadcasted_iota(jnp.int32, (fine, columns), 0)
    odd = lax.broadcasted_iota(jnp.int32, (fine, columns), 1) % 2
    q_coarse = lax.rem(at_coarse * wave, total_pitch)
    q_fine = lax.rem(at_fine * wave - odd * (total_pitch // 4), total_pitch)
    a = step * q_coarse.astype(jnp.float32)
    b = step * q_fine.astype(jnp.float32) + turn
    return jnp.cos(a), jnp.sin(a), jnp.cos(b), jnp.sin(b)


def fill_table(ref, at, factors, scale):
    cos_a, sin_a, cos_b, sin_b = factors
    fine = cos_b.shape[0]
    cos_b = cos_b * scale
    sin_b = sin_b * scale
    for i in range(cos_a.shape[0]):
        value = cos_a[i : i + 1] * cos_b - sin_a[i : i + 1] * sin_b
        ref[at + (pl.ds(i * fine, fine), slice(None))] = value.astype(ref.dtype)


def geometry(outlet_shape, stator_rows):
    rows = outlet_shape[-2]
    total_rows = 2 * rows
    rs_loc = stator_rows // 2
    slope = (stator_rows - 1) / (total_rows - BAND)
    above = math.floor((rows - 1 + JITTER) * slope) + 1 - rs_loc
    below = rs_loc - math.ceil((rows - BAND + 1 - JITTER) * slope)
    halo = -(-max(above, below) // 16) * 16
    reach = max(
        rows - math.floor(rs_loc / slope - JITTER),
        math.floor((rs_loc - 1) / slope + JITTER) + BAND - rows,
    )
    edge = -(-reach // LANES) * LANES
    return rs_loc, halo, edge


def window(first, number):
    starts = [at // LANES * LANES for at in first]
    width = max(-(-(at + number) // LANES) * LANES - start for at, start in zip(first, starts))
    return starts, width


def by_span(span_at, values, multiple):
    return pl.multiple_of(jnp.where(span_at == 0, values[0], values[1]), multiple)


def flip_weights(weight_ref, starts_ref, first_row, first_column, flipped):
    rows, width = weight_ref.shape
    row = first_row + lax.broadcasted_iota(jnp.int32, (rows, LANES), 0)
    for block in range(width // LANES):
        start = starts_ref[pl.ds(first_column // LANES + block, 1), :]
        inside = (row >= start) & (row < start + BAND)
        at = slice(block * LANES, (block + 1) * LANES)
        value = jnp.where(inside, weight_ref[:, at].astype(jnp.float32), 0.0)
        flipped[at, :] = value.T.astype(flipped.dtype)


def instance_turn(wave, instance, period):
    whole = period.astype(jnp.float32)
    steps = (wave * instance).astype(jnp.float32)
    return (2.0 * math.pi) * (steps - whole * jnp.floor(steps / whole)) / whole


def fill_analysis(wave, counts_ref, part, instances, total_pitch, table_ref):
    pitch = table_ref.shape[0]
    instance = lax.axis_index("row") * instances + part
    period = lax.axis_size("row") * instances * counts_ref[0]
    turn = instance_turn(wave, instance, period)
    factors = table_factors(wave, lax.axis_index("pitch") * pitch, pitch, total_pitch, turn)
    fill_table(table_ref, (), factors, math.sqrt(2.0 / total_pitch))


def started(*copies):
    for copy in copies:
        copy.start()
    return copies


def edge_kernel(
    sizes, counts_hbm, orders_hbm, starts_hbm, weight_hbm, planes_hbm, *rest,
):
    instances, fields, rs_loc, halo, edge, total_pitch = sizes
    halo_refs, (table_ref, planes_ref) = rest[:instances], rest[instances : instances + 2]
    counts, orders, starts, weight, edges, flipped, spectra, sems, plane_sems = rest[
        instances + 2 :
    ]
    rows, pitch = planes_hbm.shape[1:]
    others = rows - edge
    span_at = lax.axis_index("span")
    first_halo = (rs_loc, rs_loc - halo)
    columns, width = window(first_halo, halo)
    first_row = pl.multiple_of((1 - span_at) * (rows - edge), 16)
    first_column = by_span(span_at, columns, LANES)
    small = started(
        pltpu.make_async_copy(counts_hbm, counts, sems.at[0]),
        pltpu.make_async_copy(orders_hbm, orders, sems.at[1]),
        pltpu.make_async_copy(starts_hbm, starts, sems.at[2]),
        pltpu.make_async_copy(
            weight_hbm.at[pl.ds(first_row, edge), pl.ds(first_column, width)], weight, sems.at[3]
        ),
    )
    edge_rows = pl.ds(first_row, edge)
    other_rows = pl.ds(pl.multiple_of(span_at * edge, 16), others)
    fetched = started(
        pltpu.make_async_copy(
            planes_hbm.at[pl.ds(0, fields), edge_rows, :],
            planes_ref.at[:, edge_rows, :],
            plane_sems.at[0],
        ),
        *(
            pltpu.make_async_copy(
                planes_hbm.at[pl.ds(j * fields, fields), edge_rows, :],
                edges.at[j - 1],
                plane_sems.at[j],
            )
            for j in range(1, instances)
        ),
    )
    (rest_fetched,) = started(
        pltpu.make_async_copy(
            planes_hbm.at[pl.ds(0, fields), other_rows, :],
            planes_ref.at[:, other_rows, :],
            plane_sems.at[instances],
        )
    )
    for copy in small[:2]:
        copy.wait()
    wave = column_wavenumbers(counts, orders)
    for j in range(instances):
        fill_analysis(wave, counts, j, instances, total_pitch, table_ref.at[j])
    for copy in small[2:]:
        copy.wait()
    flip_weights(weight, starts, span_at * rows + first_row, first_column, flipped)
    inner = [first - start for first, start in zip(first_halo, columns)]
    weights = flipped[pl.ds(by_span(span_at, inner, 16), halo), :]
    number = table_ref.shape[2]
    for j in range(instances):
        fetched[j].wait()
        taken = planes_ref[:, edge_rows, :] if j == 0 else edges[j - 1]
        result = jnp.dot(
            taken.reshape(fields * edge, pitch),
            table_ref[j],
            preferred_element_type=jnp.float32,
        ).astype(jnp.bfloat16)
        for f in range(fields):
            at = (j * fields + f) * number
            spectra[:, at : at + number] = result[f * edge : (f + 1) * edge]
    result = jnp.dot(weights, spectra[...], preferred_element_type=jnp.float32)
    for j in range(instances):
        for f in range(fields):
            at = (j * fields + f) * number
            halo_refs[j][f] = result[:, at : at + number].astype(jnp.bfloat16)
    rest_fetched.wait()


def edge_call(sizes, counts, orders, starts, weight, planes):
    instances, fields, rs_loc, halo, edge, total_pitch = sizes
    pitch = planes.shape[2]
    columns = 2 * orders.shape[1]
    width = window((rs_loc, rs_loc - halo), halo)[1]
    count = instances * fields
    vmem = pl.BlockSpec(memory_space=pltpu.VMEM)
    hbm = pl.BlockSpec(memory_space=pltpu.HBM)
    return pl.pallas_call(
        functools.partial(edge_kernel, sizes),
        out_shape=[jax.ShapeDtypeStruct((fields, halo, columns), jnp.bfloat16)] * instances
        + [
            jax.ShapeDtypeStruct((instances, pitch, columns), jnp.bfloat16),
            pltpu.VMEM((fields, *planes.shape[1:]), jnp.bfloat16),
        ],
        in_specs=[hbm] * 5,
        out_specs=[vmem] * (instances + 2),
        scratch_shapes=[
            pltpu.SMEM(counts.shape, jnp.int32),
            pltpu.VMEM(orders.shape, jnp.int32),
            pltpu.VMEM(starts.shape, jnp.int32),
            pltpu.VMEM((edge, width), jnp.bfloat16),
            pltpu.VMEM((max(instances - 1, 1), fields, edge, pitch), jnp.bfloat16),
            pltpu.VMEM((width, edge), jnp.bfloat16),
            pltpu.VMEM((edge, count * columns), jnp.bfloat16),
            pltpu.SemaphoreType.DMA((4,)),
            pltpu.SemaphoreType.DMA((instances + 1,)),
        ],
        compiler_params=pltpu.CompilerParams(vmem_limit_bytes=VMEM_BYTES),
        cost_estimate=pl.CostEstimate(
            flops=2 * count * edge * columns * (pitch + halo),
            bytes_accessed=2 * count * edge * pitch,
            transcendentals=0,
        ),
        name="edge",
    )(counts, orders, starts, weight, planes)


def analyse_planes(planes_ref, table_ref, band_ref, spectra, out_refs):
    fields, rows, pitch = planes_ref.shape
    columns = table_ref.shape[1]
    per = band_ref.shape[0] // len(out_refs)
    result = jnp.dot(
        planes_ref[...].reshape(fields * rows, pitch),
        table_ref[...],
        preferred_element_type=jnp.float32,
    ).astype(jnp.bfloat16)
    for f in range(fields):
        spectra[:, f * columns : (f + 1) * columns] = result[f * rows : (f + 1) * rows]
    result = jnp.dot(band_ref[...], spectra[...], preferred_element_type=jnp.float32)
    for k, out_ref in enumerate(out_refs):
        for f in range(fields):
            out_ref[f] = result[
                k * per : (k + 1) * per, f * columns : (f + 1) * columns
            ].astype(out_ref.dtype)


def next_planes(planes_hbm, part, next_ref, sem):
    return pltpu.make_async_copy(
        planes_hbm.at[pl.ds((part + 1) * next_ref.shape[0], next_ref.shape[0])], next_ref, sem
    )


def first_kernel(
    sizes, shards, starts_hbm, weight_hbm, planes_hbm, planes_ref, table_ref, *rest,
):
    instances, fields, rs_loc, halo, edge, total_pitch = sizes
    out_refs, band_ref, next_refs = rest[:shards], rest[shards], rest[shards + 1 : -5]
    starts, weight, flipped, spectra, sems = rest[-5:]
    rows = weight_hbm.shape[0]
    per = rs_loc // shards
    span_at = lax.axis_index("span")
    pitch_at = lax.axis_index("pitch")
    columns, width = window((0, rs_loc), rs_loc)
    first_column = by_span(span_at, columns, LANES)
    small = started(
        pltpu.make_async_copy(starts_hbm, starts, sems.at[0]),
        pltpu.make_async_copy(weight_hbm.at[:, pl.ds(first_column, width)], weight, sems.at[1]),
    )
    following = started(*(next_planes(planes_hbm, 0, ref, sems.at[2]) for ref in next_refs))
    for copy in small:
        copy.wait()
    flip_weights(weight, starts, span_at * rows, first_column, flipped)
    own = by_span(span_at, (0, rs_loc - columns[1]), 16)
    for k in range(shards):
        at = jnp.bitwise_xor(pitch_at, k) if shards > 1 else 0
        source = pl.multiple_of(own + at * per, 16)
        band_ref[k * per : (k + 1) * per] = flipped[pl.ds(source, per), :]
    analyse_planes(planes_ref, table_ref.at[0], band_ref, spectra, out_refs)
    for copy in following:
        copy.wait()


def own_shapes(shards, fields, per, columns):
    kinds = [jnp.bfloat16 if k in (1, 2) else jnp.float32 for k in range(shards)]
    return [jax.ShapeDtypeStruct((fields, per, columns), kind) for kind in kinds]


def first_call(sizes, shards, starts, weight, planes, held, table):
    instances, fields, rs_loc, halo, edge, total_pitch = sizes
    rows, pitch = planes.shape[1:]
    columns = table.shape[2]
    width = window((0, rs_loc), rs_loc)[1]
    vmem = pl.BlockSpec(memory_space=pltpu.VMEM)
    hbm = pl.BlockSpec(memory_space=pltpu.HBM)
    following = [pltpu.VMEM((fields, rows, pitch), jnp.bfloat16)] * (instances > 1)
    return pl.pallas_call(
        functools.partial(first_kernel, sizes, shards),
        out_shape=own_shapes(shards, fields, rs_loc // shards, columns)
        + [jax.ShapeDtypeStruct((rs_loc, rows), jnp.bfloat16)]
        + following,
        in_specs=[hbm, hbm, hbm, vmem, vmem],
        out_specs=[vmem] * (shards + 1 + len(following)),
        scratch_shapes=[
            pltpu.VMEM(starts.shape, jnp.int32),
            pltpu.VMEM((rows, width), jnp.bfloat16),
            pltpu.VMEM((width, rows), jnp.bfloat16),
            pltpu.VMEM((rows, fields * columns), jnp.bfloat16),
            pltpu.SemaphoreType.DMA((3,)),
        ],
        compiler_params=pltpu.CompilerParams(vmem_limit_bytes=VMEM_BYTES),
        cost_estimate=pl.CostEstimate(
            flops=2 * fields * rows * columns * (pitch + rs_loc),
            bytes_accessed=2 * fields * rows * pitch,
            transcendentals=0,
        ),
        name="first_part",
    )(starts, weight, planes, held, table)


def later_kernel(
    sizes, shards, part,
    counts_hbm, orders_hbm, planes_hbm, planes_ref, table_ref, band_ref, after_ref, *rest,
):
    out_refs, synthesis_ref, next_refs = rest[:shards], rest[shards], rest[shards + 1 : -4]
    counts, orders, spectra, sems = rest[-4:]
    small = started(
        pltpu.make_async_copy(counts_hbm, counts, sems.at[0]),
        pltpu.make_async_copy(orders_hbm, orders, sems.at[1]),
    )
    following = started(*(next_planes(planes_hbm, part, ref, sems.at[2]) for ref in next_refs))
    analyse_planes(planes_ref, table_ref.at[part], band_ref, spectra, out_refs)
    for copy in small:
        copy.wait()
    wave = column_wavenumbers(counts, orders)
    pitch = synthesis_ref.shape[0]
    factors = table_factors(wave, lax.axis_index("pitch") * pitch, pitch, sizes[-1], 0.0)
    fill_table(synthesis_ref, (), factors, 1.0 / math.sqrt(wave.shape[1] // 2))
    for copy in following:
        copy.wait()


def later_call(sizes, shards, part, counts, orders, planes, held, table, band, after):
    instances, fields, rs_loc, halo, edge, total_pitch = sizes
    rows, pitch = planes.shape[1:]
    columns = table.shape[2]
    vmem = pl.BlockSpec(memory_space=pltpu.VMEM)
    hbm = pl.BlockSpec(memory_space=pltpu.HBM)
    following = [pltpu.VMEM((fields, rows, pitch), jnp.bfloat16)] * (part + 1 < instances)
    return pl.pallas_call(
        functools.partial(later_kernel, sizes, shards, part),
        out_shape=own_shapes(shards, fields, rs_loc // shards, columns)
        + [jax.ShapeDtypeStruct((pitch, columns), jnp.bfloat16)]
        + following,
        in_specs=[hbm, hbm, hbm, vmem, vmem, vmem, pl.BlockSpec(memory_space=pl.ANY)],
        out_specs=[vmem] * (shards + 1 + len(following)),
        scratch_shapes=[
            pltpu.SMEM(counts.shape, jnp.int32),
            pltpu.VMEM(orders.shape, jnp.int32),
            pltpu.VMEM((rows, fields * columns), jnp.bfloat16),
            pltpu.SemaphoreType.DMA((3,)),
        ],
        compiler_params=pltpu.CompilerParams(vmem_limit_bytes=VMEM_BYTES),
        cost_estimate=pl.CostEstimate(
            flops=2 * fields * rows * columns * (pitch + rs_loc),
            bytes_accessed=2 * fields * rows * pitch,
            transcendentals=0,
        ),
        name="later_part",
    )(counts, orders, planes, held, table, band, after)


def synthesise_kernel(fields, ranks, shards, per, table_ref, *rest):
    piece_refs = rest[: len(ranks)]
    out_hbm, rows_ref, sems = rest[-3:]
    pitch_at = lax.axis_index("pitch")
    copies = []
    for i, (part, k) in enumerate(ranks):
        piece = piece_refs[i][...]
        value = lax.dot_general(
            piece.reshape(fields * per, piece.shape[2]),
            table_ref[...],
            (((1,), (1,)), ((), ())),
            preferred_element_type=jnp.float32,
        )
        rows_ref[i] = value.astype(rows_ref.dtype).reshape(fields, per, value.shape[1])
        at = jnp.bitwise_xor(pitch_at, k) if shards > 1 else 0
        copies += started(
            pltpu.make_async_copy(
                rows_ref.at[i],
                out_hbm.at[
                    pl.ds(part * fields, fields), pl.ds(pl.multiple_of(at * per, 16), per), :
                ],
                sems.at[i],
            )
        )
    for copy in copies:
        copy.wait()


def synthesise_call(count, shards, table, pieces, base):
    ranks = list(pieces)
    fields, per, columns = pieces[ranks[0]].shape
    pitch = table.shape[0]
    vmem = pl.BlockSpec(memory_space=pltpu.VMEM)
    hbm = pl.BlockSpec(memory_space=pltpu.HBM)
    operands = [table, *pieces.values()]
    in_specs = [vmem] * len(operands)
    aliases = {}
    if base is not None:
        aliases = {len(operands): 0}
        operands.append(base)
        in_specs.append(hbm)
    return pl.pallas_call(
        functools.partial(synthesise_kernel, fields, ranks, shards, per),
        out_shape=jax.ShapeDtypeStruct((count, per * shards, pitch), jnp.bfloat16),
        in_specs=in_specs,
        out_specs=hbm,
        scratch_shapes=[
            pltpu.VMEM((len(ranks), fields, per, pitch), jnp.bfloat16),
            pltpu.SemaphoreType.DMA((len(ranks),)),
        ],
        input_output_aliases=aliases,
        compiler_params=pltpu.CompilerParams(vmem_limit_bytes=VMEM_BYTES),
        cost_estimate=pl.CostEstimate(
            flops=2 * len(ranks) * fields * per * columns * pitch,
            bytes_accessed=2 * len(ranks) * fields * per * pitch,
            transcendentals=0,
        ),
        name="synthesise",
    )(*operands)


def body(outlet, remap_weight, band_start, blade_counts, mode_orders):
    row_count = lax.axis_size("row")
    pitch_count = lax.axis_size("pitch")
    instances, fields, rows, pitch = outlet.shape[1:]
    stator_rows = remap_weight.shape[1]
    total_pitch = pitch * pitch_count
    rs_loc, halo_rows, edge = geometry(outlet.shape, stator_rows)
    count = instances * fields
    by_shards = (
        pitch_count == 4
        and rs_loc % (16 * pitch_count) == 0
        and halo_rows == rs_loc // pitch_count
    )
    shards = pitch_count if by_shards else 1
    shift = row_count // 2

    def stay(value):
        return pltpu.with_memory_space_constraint(value, pltpu.HBM)

    planes = stay(outlet.reshape(count, rows, pitch))
    orders = stay(mode_orders.T)
    starts = stay(band_start.reshape(stator_rows // LANES, LANES))
    blade_counts = stay(blade_counts)
    remap_weight = stay(remap_weight)
    sizes = (instances, fields, rs_loc, halo_rows, edge, total_pitch)
    halo_at = jnp.where(lax.axis_index("span") == 0, shards - 1, 0)
    holds = [jnp.bitwise_xor(lax.axis_index("pitch"), k) == halo_at for k in range(shards)]
    *halos, table, held = edge_call(
        sizes, after(blade_counts, *holds), orders, starts, remap_weight, planes
    )
    made = first_call(sizes, shards, starts, remap_weight, planes, held, table)
    owns, band, held = [made[:shards]], made[shards], made[-1]
    known = {}

    def get(kind, part):
        if (kind, part) not in known:
            known[kind, part] = steps[kind](part)
        return known[kind, part]

    def ready(kind, part, value):
        return after(value, *(get(*step) for step in ORDER.get((kind, part), ())))

    def later(part):
        if part == 0:
            return owns[0][-1]
        first_sent = halos[0] if shards == 1 else get("meet", 0)[1]
        made = later_call(
            sizes, shards, part, blade_counts, orders, planes,
            known.get(("held", part), held), table, band, ready("later", part, first_sent),
        )
        owns.append(made[:shards])
        known["synthesis", 0] = made[shards]
        known["held", part + 1] = made[-1]
        return made[0]

    def halo(part):
        return exchange(ready("halo", part, halos[part]), "span", 1)

    def with_halo(part, k, *terms):
        get("later", part)
        total = jnp.where(holds[k], get("halo", part).astype(jnp.float32), 0.0)
        for term in (owns[part][k], *terms):
            total = total + term.astype(jnp.float32)
        return total.astype(jnp.bfloat16)

    def meet(part):
        return None, with_halo(part, 2)

    def pair_sent(part):
        sent = [get("meet", part)[1]]
        if JOIN == 2:
            sent.append(with_halo(part, 1))
        elif part > 0 and JOIN:
            sent.append(with_halo(part - 1, 1))
        return exchange(ready("pair", part, jnp.stack(sent)), "pitch", 1)

    def pair(part):
        return get("pair_sent", part)[0]

    def beside(part):
        if JOIN == 2:
            return get("pair_sent", part)[1]
        if part + 1 < instances and JOIN:
            return get("pair_sent", part + 1)[1]
        return exchange(ready("beside", part, with_halo(part, 1)), "pitch", 1)

    def across(part):
        return exchange(
            ready("across", part, with_halo(part, 3, get("pair", part))), "pitch", 3
        )

    def total(part):
        return with_halo(part, 0, get("beside", part), get("across", part))

    def spread(value, k):
        pairs = [
            (g * pitch_count + z, ((g + shift) % row_count) * pitch_count + (z ^ k))
            for g in range(row_count)
            for z in range(pitch_count)
        ]
        return lax.ppermute(value, ("row", "pitch"), pairs)

    def swap(part):
        return spread(ready("swap", part, get("total", part)), 0)

    def swap_across(part):
        return spread(ready("swap_across", part, get("total", part)), 3)

    def swap_beside(part):
        if part in DIRECT:
            return spread(ready("swap_beside", part, get("total", part)), 1)
        return exchange(ready("swap_beside", part, get("swap", part)), "pitch", 1)

    def across_on(part):
        return exchange(ready("across_on", part, get("swap_across", part)), "pitch", 1)

    def synth(at):
        base = get("synth", at - 1) if at else None
        group = {(part, k): get(names[k], part) for part, k in GROUPS[at]}
        return synthesise_call(count, shards, known["synthesis", 0], group, base)

    steps = dict(
        synth=synth,
        later=later, halo=halo, meet=meet, pair_sent=pair_sent, pair=pair, beside=beside, across=across, total=total,
        swap=swap, swap_across=swap_across, swap_beside=swap_beside, across_on=across_on,
    )
    names = ("swap", "swap_beside", "across_on", "swap_across")

    def whole_sum(part):
        get("later", part)
        wide = get("halo", part).astype(jnp.float32)
        low = jnp.pad(wide, ((0, 0), (rs_loc - halo_rows, 0), (0, 0)))
        high = jnp.pad(wide, ((0, 0), (0, rs_loc - halo_rows), (0, 0)))
        mine = owns[part][0] + jnp.where(lax.axis_index("span") == 0, low, high)
        return lax.psum(mine, "pitch").astype(jnp.bfloat16)

    joined = None
    get("later", instances - 1)
    if by_shards:
        joined = get("synth", len(GROUPS) - 1)
    else:
        pairs = [(g, (g + shift) % row_count) for g in range(row_count)]
        pieces = {
            (part, 0): lax.ppermute(whole_sum(part), "row", pairs) for part in range(instances)
        }
        joined = synthesise_call(count, shards, known["synthesis", 0], pieces, joined)
    return joined.reshape(1, instances, fields, rs_loc, pitch)


def solution(mesh):
    placed = (P("row", None, None, "span", "pitch"), P("span", None), P(), P(), P())
    return jax.shard_map(
        body,
        mesh=mesh,
        in_specs=placed,
        out_specs=P("row", None, None, "span", "pitch"),
        check_vma=False,
    )
```

```python
import functools
import math

import jax
import jax.numpy as jnp
from jax import lax
from jax.experimental import pallas as pl
from jax.experimental.pallas import tpu as pltpu
from jax.sharding import PartitionSpec as P

BAND = 192
JITTER = 6
LANES = 128
ORDER = {}
JOIN = 0
DIRECT = (1,)
GROUPS = (((0, 0), (0, 3)), ((1, 0), (1, 3), (0, 1), (0, 2)), ((1, 1), (1, 2)))
VMEM_BYTES = 32 * 1024 * 1024


def exchange(value, axis, distance):
    count = lax.axis_size(axis)
    return lax.ppermute(value, axis, [(i, i ^ distance) for i in range(count)])


def after(value, *others):
    return lax.optimization_barrier((value, *others))[0] if others else value


def column_wavenumbers(counts_ref, orders_ref):
    harmonics = orders_ref.shape[1]
    columns = 2 * harmonics
    spread = (
        lax.broadcasted_iota(jnp.int32, (harmonics, columns), 1) // 2
        == lax.broadcasted_iota(jnp.int32, (harmonics, columns), 0)
    )
    orders = jnp.dot(
        orders_ref[...].astype(jnp.float32),
        spread.astype(jnp.float32),
        preferred_element_type=jnp.float32,
    ).astype(jnp.int32)
    return orders[0:1] * counts_ref[0] + orders[1:2] * counts_ref[1]


def table_factors(wave, first_row, rows, total_pitch, turn):
    fine = 32
    coarse = rows // fine
    columns = wave.shape[1]
    step = 2.0 * math.pi / total_pitch
    at_coarse = first_row + fine * lax.broadcasted_iota(jnp.int32, (coarse, columns), 0)
    at_fine = lax.broadcasted_iota(jnp.int32, (fine, columns), 0)
    odd = lax.broadcasted_iota(jnp.int32, (fine, columns), 1) % 2
    q_coarse = lax.rem(at_coarse * wave, total_pitch)
    q_fine = lax.rem(at_fine * wave - odd * (total_pitch // 4), total_pitch)
    a = step * q_coarse.astype(jnp.float32)
    b = step * q_fine.astype(jnp.float32) + turn
    return jnp.cos(a), jnp.sin(a), jnp.cos(b), jnp.sin(b)


def fill_table(ref, at, factors, scale):
    cos_a, sin_a, cos_b, sin_b = factors
    fine = cos_b.shape[0]
    cos_b = cos_b * scale
    sin_b = sin_b * scale
    for i in range(cos_a.shape[0]):
        value = cos_a[i : i + 1] * cos_b - sin_a[i : i + 1] * sin_b
        ref[at + (pl.ds(i * fine, fine), slice(None))] = value.astype(ref.dtype)


def geometry(outlet_shape, stator_rows):
    rows = outlet_shape[-2]
    total_rows = 2 * rows
    rs_loc = stator_rows // 2
    slope = (stator_rows - 1) / (total_rows - BAND)
    above = math.floor((rows - 1 + JITTER) * slope) + 1 - rs_loc
    below = rs_loc - math.ceil((rows - BAND + 1 - JITTER) * slope)
    halo = -(-max(above, below) // 16) * 16
    reach = max(
        rows - math.floor(rs_loc / slope - JITTER),
        math.floor((rs_loc - 1) / slope + JITTER) + BAND - rows,
    )
    edge = -(-reach // LANES) * LANES
    return rs_loc, halo, edge


def window(first, number):
    starts = [at // LANES * LANES for at in first]
    width = max(-(-(at + number) // LANES) * LANES - start for at, start in zip(first, starts))
    return starts, width


def by_span(span_at, values, multiple):
    return pl.multiple_of(jnp.where(span_at == 0, values[0], values[1]), multiple)


def flip_weights(weight_ref, starts_ref, first_row, first_column, flipped):
    rows, width = weight_ref.shape
    row = first_row + lax.broadcasted_iota(jnp.int32, (rows, LANES), 0)
    for block in range(width // LANES):
        start = starts_ref[pl.ds(first_column // LANES + block, 1), :]
        inside = (row >= start) & (row < start + BAND)
        at = slice(block * LANES, (block + 1) * LANES)
        value = jnp.where(inside, weight_ref[:, at].astype(jnp.float32), 0.0)
        flipped[at, :] = value.T.astype(flipped.dtype)


def instance_turn(wave, instance, period):
    whole = period.astype(jnp.float32)
    steps = (wave * instance).astype(jnp.float32)
    return (2.0 * math.pi) * (steps - whole * jnp.floor(steps / whole)) / whole


def fill_analysis(wave, counts_ref, part, instances, total_pitch, table_ref):
    pitch = table_ref.shape[0]
    instance = lax.axis_index("row") * instances + part
    period = lax.axis_size("row") * instances * counts_ref[0]
    turn = instance_turn(wave, instance, period)
    factors = table_factors(wave, lax.axis_index("pitch") * pitch, pitch, total_pitch, turn)
    fill_table(table_ref, (), factors, math.sqrt(2.0 / total_pitch))


def started(*copies):
    for copy in copies:
        copy.start()
    return copies


def edge_kernel(
    sizes, counts_hbm, orders_hbm, starts_hbm, weight_hbm, planes_hbm, *rest,
):
    instances, fields, rs_loc, halo, edge, total_pitch = sizes
    halo_refs, (table_ref, planes_ref) = rest[:instances], rest[instances : instances + 2]
    counts, orders, starts, weight, edges, flipped, spectra, sems, plane_sems = rest[
        instances + 2 :
    ]
    rows, pitch = planes_hbm.shape[1:]
    others = rows - edge
    span_at = lax.axis_index("span")
    first_halo = (rs_loc, rs_loc - halo)
    columns, width = window(first_halo, halo)
    first_row = pl.multiple_of((1 - span_at) * (rows - edge), 16)
    first_column = by_span(span_at, columns, LANES)
    small = started(
        pltpu.make_async_copy(counts_hbm, counts, sems.at[0]),
        pltpu.make_async_copy(orders_hbm, orders, sems.at[1]),
        pltpu.make_async_copy(starts_hbm, starts, sems.at[2]),
        pltpu.make_async_copy(
            weight_hbm.at[pl.ds(first_row, edge), pl.ds(first_column, width)], weight, sems.at[3]
        ),
    )
    edge_rows = pl.ds(first_row, edge)
    other_rows = pl.ds(pl.multiple_of(span_at * edge, 16), others)
    fetched = started(
        pltpu.make_async_copy(
            planes_hbm.at[pl.ds(0, fields), edge_rows, :],
            planes_ref.at[:, edge_rows, :],
            plane_sems.at[0],
        ),
        *(
            pltpu.make_async_copy(
                planes_hbm.at[pl.ds(j * fields, fields), edge_rows, :],
                edges.at[j - 1],
                plane_sems.at[j],
            )
            for j in range(1, instances)
        ),
    )
    (rest_fetched,) = started(
        pltpu.make_async_copy(
            planes_hbm.at[pl.ds(0, fields), other_rows, :],
            planes_ref.at[:, other_rows, :],
            plane_sems.at[instances],
        )
    )
    for copy in small[:2]:
        copy.wait()
    wave = column_wavenumbers(counts, orders)
    for j in range(instances):
        fill_analysis(wave, counts, j, instances, total_pitch, table_ref.at[j])
    for copy in small[2:]:
        copy.wait()
    flip_weights(weight, starts, span_at * rows + first_row, first_column, flipped)
    inner = [first - start for first, start in zip(first_halo, columns)]
    weights = flipped[pl.ds(by_span(span_at, inner, 16), halo), :]
    number = table_ref.shape[2]
    for j in range(instances):
        fetched[j].wait()
        taken = planes_ref[:, edge_rows, :] if j == 0 else edges[j - 1]
        result = jnp.dot(
            taken.reshape(fields * edge, pitch),
            table_ref[j],
            preferred_element_type=jnp.float32,
        ).astype(jnp.bfloat16)
        for f in range(fields):
            at = (j * fields + f) * number
            spectra[:, at : at + number] = result[f * edge : (f + 1) * edge]
    result = jnp.dot(weights, spectra[...], preferred_element_type=jnp.float32)
    for j in range(instances):
        for f in range(fields):
            at = (j * fields + f) * number
            halo_refs[j][f] = result[:, at : at + number].astype(jnp.bfloat16)
    rest_fetched.wait()


def edge_call(sizes, counts, orders, starts, weight, planes):
    instances, fields, rs_loc, halo, edge, total_pitch = sizes
    pitch = planes.shape[2]
    columns = 2 * orders.shape[1]
    width = window((rs_loc, rs_loc - halo), halo)[1]
    count = instances * fields
    vmem = pl.BlockSpec(memory_space=pltpu.VMEM)
    hbm = pl.BlockSpec(memory_space=pltpu.HBM)
    return pl.pallas_call(
        functools.partial(edge_kernel, sizes),
        out_shape=[jax.ShapeDtypeStruct((fields, halo, columns), jnp.bfloat16)] * instances
        + [
            jax.ShapeDtypeStruct((instances, pitch, columns), jnp.bfloat16),
            pltpu.VMEM((fields, *planes.shape[1:]), jnp.bfloat16),
        ],
        in_specs=[hbm] * 5,
        out_specs=[vmem] * (instances + 2),
        scratch_shapes=[
            pltpu.SMEM(counts.shape, jnp.int32),
            pltpu.VMEM(orders.shape, jnp.int32),
            pltpu.VMEM(starts.shape, jnp.int32),
            pltpu.VMEM((edge, width), jnp.bfloat16),
            pltpu.VMEM((max(instances - 1, 1), fields, edge, pitch), jnp.bfloat16),
            pltpu.VMEM((width, edge), jnp.bfloat16),
            pltpu.VMEM((edge, count * columns), jnp.bfloat16),
            pltpu.SemaphoreType.DMA((4,)),
            pltpu.SemaphoreType.DMA((instances + 1,)),
        ],
        compiler_params=pltpu.CompilerParams(vmem_limit_bytes=VMEM_BYTES),
        cost_estimate=pl.CostEstimate(
            flops=2 * count * edge * columns * (pitch + halo),
            bytes_accessed=2 * count * edge * pitch,
            transcendentals=0,
        ),
        name="edge",
    )(counts, orders, starts, weight, planes)


def analyse_planes(planes_ref, table_ref, band_ref, spectra, out_refs):
    fields, rows, pitch = planes_ref.shape
    columns = table_ref.shape[1]
    per = band_ref.shape[0] // len(out_refs)
    result = jnp.dot(
        planes_ref[...].reshape(fields * rows, pitch),
        table_ref[...],
        preferred_element_type=jnp.float32,
    ).astype(jnp.bfloat16)
    for f in range(fields):
        spectra[:, f * columns : (f + 1) * columns] = result[f * rows : (f + 1) * rows]
    result = jnp.dot(band_ref[...], spectra[...], preferred_element_type=jnp.float32)
    for k, out_ref in enumerate(out_refs):
        for f in range(fields):
            out_ref[f] = result[
                k * per : (k + 1) * per, f * columns : (f + 1) * columns
            ].astype(out_ref.dtype)


def next_planes(planes_hbm, part, next_ref, sem):
    return pltpu.make_async_copy(
        planes_hbm.at[pl.ds((part + 1) * next_ref.shape[0], next_ref.shape[0])], next_ref, sem
    )


def first_kernel(
    sizes, shards, starts_hbm, weight_hbm, planes_hbm, planes_ref, table_ref, *rest,
):
    instances, fields, rs_loc, halo, edge, total_pitch = sizes
    out_refs, band_ref, next_refs = rest[:shards], rest[shards], rest[shards + 1 : -5]
    starts, weight, flipped, spectra, sems = rest[-5:]
    rows = weight_hbm.shape[0]
    per = rs_loc // shards
    span_at = lax.axis_index("span")
    pitch_at = lax.axis_index("pitch")
    columns, width = window((0, rs_loc), rs_loc)
    first_column = by_span(span_at, columns, LANES)
    small = started(
        pltpu.make_async_copy(starts_hbm, starts, sems.at[0]),
        pltpu.make_async_copy(weight_hbm.at[:, pl.ds(first_column, width)], weight, sems.at[1]),
    )
    following = started(*(next_planes(planes_hbm, 0, ref, sems.at[2]) for ref in next_refs))
    for copy in small:
        copy.wait()
    flip_weights(weight, starts, span_at * rows, first_column, flipped)
    own = by_span(span_at, (0, rs_loc - columns[1]), 16)
    for k in range(shards):
        at = jnp.bitwise_xor(pitch_at, k) if shards > 1 else 0
        source = pl.multiple_of(own + at * per, 16)
        band_ref[k * per : (k + 1) * per] = flipped[pl.ds(source, per), :]
    analyse_planes(planes_ref, table_ref.at[0], band_ref, spectra, out_refs)
    for copy in following:
        copy.wait()


def own_shapes(shards, fields, per, columns):
    kinds = [jnp.bfloat16 if k in (1, 2) else jnp.float32 for k in range(shards)]
    return [jax.ShapeDtypeStruct((fields, per, columns), kind) for kind in kinds]


def first_call(sizes, shards, starts, weight, planes, held, table):
    instances, fields, rs_loc, halo, edge, total_pitch = sizes
    rows, pitch = planes.shape[1:]
    columns = table.shape[2]
    width = window((0, rs_loc), rs_loc)[1]
    vmem = pl.BlockSpec(memory_space=pltpu.VMEM)
    hbm = pl.BlockSpec(memory_space=pltpu.HBM)
    following = [pltpu.VMEM((fields, rows, pitch), jnp.bfloat16)] * (instances > 1)
    return pl.pallas_call(
        functools.partial(first_kernel, sizes, shards),
        out_shape=own_shapes(shards, fields, rs_loc // shards, columns)
        + [jax.ShapeDtypeStruct((rs_loc, rows), jnp.bfloat16)]
        + following,
        in_specs=[hbm, hbm, hbm, vmem, vmem],
        out_specs=[vmem] * (shards + 1 + len(following)),
        scratch_shapes=[
            pltpu.VMEM(starts.shape, jnp.int32),
            pltpu.VMEM((rows, width), jnp.bfloat16),
            pltpu.VMEM((width, rows), jnp.bfloat16),
            pltpu.VMEM((rows, fields * columns), jnp.bfloat16),
            pltpu.SemaphoreType.DMA((3,)),
        ],
        compiler_params=pltpu.CompilerParams(vmem_limit_bytes=VMEM_BYTES),
        cost_estimate=pl.CostEstimate(
            flops=2 * fields * rows * columns * (pitch + rs_loc),
            bytes_accessed=2 * fields * rows * pitch,
            transcendentals=0,
        ),
        name="first_part",
    )(starts, weight, planes, held, table)


def later_kernel(
    sizes, shards, part,
    counts_hbm, orders_hbm, planes_hbm, planes_ref, table_ref, band_ref, after_ref, *rest,
):
    out_refs, synthesis_ref, next_refs = rest[:shards], rest[shards], rest[shards + 1 : -4]
    counts, orders, spectra, sems = rest[-4:]
    small = started(
        pltpu.make_async_copy(counts_hbm, counts, sems.at[0]),
        pltpu.make_async_copy(orders_hbm, orders, sems.at[1]),
    )
    following = started(*(next_planes(planes_hbm, part, ref, sems.at[2]) for ref in next_refs))
    analyse_planes(planes_ref, table_ref.at[part], band_ref, spectra, out_refs)
    for copy in small:
        copy.wait()
    wave = column_wavenumbers(counts, orders)
    pitch = synthesis_ref.shape[0]
    factors = table_factors(wave, lax.axis_index("pitch") * pitch, pitch, sizes[-1], 0.0)
    fill_table(synthesis_ref, (), factors, 1.0 / math.sqrt(wave.shape[1] // 2))
    for copy in following:
        copy.wait()


def later_call(sizes, shards, part, counts, orders, planes, held, table, band, after):
    instances, fields, rs_loc, halo, edge, total_pitch = sizes
    rows, pitch = planes.shape[1:]
    columns = table.shape[2]
    vmem = pl.BlockSpec(memory_space=pltpu.VMEM)
    hbm = pl.BlockSpec(memory_space=pltpu.HBM)
    following = [pltpu.VMEM((fields, rows, pitch), jnp.bfloat16)] * (part + 1 < instances)
    return pl.pallas_call(
        functools.partial(later_kernel, sizes, shards, part),
        out_shape=own_shapes(shards, fields, rs_loc // shards, columns)
        + [jax.ShapeDtypeStruct((pitch, columns), jnp.bfloat16)]
        + following,
        in_specs=[hbm, hbm, hbm, vmem, vmem, vmem, pl.BlockSpec(memory_space=pl.ANY)],
        out_specs=[vmem] * (shards + 1 + len(following)),
        scratch_shapes=[
            pltpu.SMEM(counts.shape, jnp.int32),
            pltpu.VMEM(orders.shape, jnp.int32),
            pltpu.VMEM((rows, fields * columns), jnp.bfloat16),
            pltpu.SemaphoreType.DMA((3,)),
        ],
        compiler_params=pltpu.CompilerParams(vmem_limit_bytes=VMEM_BYTES),
        cost_estimate=pl.CostEstimate(
            flops=2 * fields * rows * columns * (pitch + rs_loc),
            bytes_accessed=2 * fields * rows * pitch,
            transcendentals=0,
        ),
        name="later_part",
    )(counts, orders, planes, held, table, band, after)


def synthesise_kernel(fields, ranks, shards, per, table_ref, *rest):
    piece_refs = rest[: len(ranks)]
    out_hbm, rows_ref, sems = rest[-3:]
    pitch_at = lax.axis_index("pitch")
    copies = []
    for i, (part, k) in enumerate(ranks):
        at = jnp.bitwise_xor(pitch_at, k) if shards > 1 else 0
        place = pl.ds(pl.multiple_of(at * per, 16), per)
        cuts = [0, (fields + 1) // 2, fields]
        for half, (low, high) in enumerate(zip(cuts, cuts[1:])):
            piece = piece_refs[i][low:high]
            value = lax.dot_general(
                piece.reshape((high - low) * per, piece.shape[2]),
                table_ref[...],
                (((1,), (1,)), ((), ())),
                preferred_element_type=jnp.float32,
            )
            rows_ref[i, low:high] = value.astype(rows_ref.dtype).reshape(high - low, per, -1)
            copies += started(
                pltpu.make_async_copy(
                    rows_ref.at[i, pl.ds(low, high - low)],
                    out_hbm.at[pl.ds(part * fields + low, high - low), place, :],
                    sems.at[i, half],
                )
            )
    for copy in copies:
        copy.wait()


def synthesise_call(count, shards, table, pieces, base):
    ranks = list(pieces)
    fields, per, columns = pieces[ranks[0]].shape
    pitch = table.shape[0]
    vmem = pl.BlockSpec(memory_space=pltpu.VMEM)
    hbm = pl.BlockSpec(memory_space=pltpu.HBM)
    operands = [table, *pieces.values()]
    in_specs = [vmem] * len(operands)
    aliases = {}
    if base is not None:
        aliases = {len(operands): 0}
        operands.append(base)
        in_specs.append(hbm)
    return pl.pallas_call(
        functools.partial(synthesise_kernel, fields, ranks, shards, per),
        out_shape=jax.ShapeDtypeStruct((count, per * shards, pitch), jnp.bfloat16),
        in_specs=in_specs,
        out_specs=hbm,
        scratch_shapes=[
            pltpu.VMEM((len(ranks), fields, per, pitch), jnp.bfloat16),
            pltpu.SemaphoreType.DMA((len(ranks), 2)),
        ],
        input_output_aliases=aliases,
        compiler_params=pltpu.CompilerParams(vmem_limit_bytes=VMEM_BYTES),
        cost_estimate=pl.CostEstimate(
            flops=2 * len(ranks) * fields * per * columns * pitch,
            bytes_accessed=2 * len(ranks) * fields * per * pitch,
            transcendentals=0,
        ),
        name="synthesise",
    )(*operands)


def body(outlet, remap_weight, band_start, blade_counts, mode_orders):
    row_count = lax.axis_size("row")
    pitch_count = lax.axis_size("pitch")
    instances, fields, rows, pitch = outlet.shape[1:]
    stator_rows = remap_weight.shape[1]
    total_pitch = pitch * pitch_count
    rs_loc, halo_rows, edge = geometry(outlet.shape, stator_rows)
    count = instances * fields
    by_shards = (
        pitch_count == 4
        and rs_loc % (16 * pitch_count) == 0
        and halo_rows == rs_loc // pitch_count
    )
    shards = pitch_count if by_shards else 1
    shift = row_count // 2

    def stay(value):
        return pltpu.with_memory_space_constraint(value, pltpu.HBM)

    planes = stay(outlet.reshape(count, rows, pitch))
    orders = stay(mode_orders.T)
    starts = stay(band_start.reshape(stator_rows // LANES, LANES))
    blade_counts = stay(blade_counts)
    remap_weight = stay(remap_weight)
    sizes = (instances, fields, rs_loc, halo_rows, edge, total_pitch)
    halo_at = jnp.where(lax.axis_index("span") == 0, shards - 1, 0)
    holds = [jnp.bitwise_xor(lax.axis_index("pitch"), k) == halo_at for k in range(shards)]
    *halos, table, held = edge_call(
        sizes, after(blade_counts, *holds), orders, starts, remap_weight, planes
    )
    made = first_call(sizes, shards, starts, remap_weight, planes, held, table)
    owns, band, held = [made[:shards]], made[shards], made[-1]
    known = {}

    def get(kind, part):
        if (kind, part) not in known:
            known[kind, part] = steps[kind](part)
        return known[kind, part]

    def ready(kind, part, value):
        return after(value, *(get(*step) for step in ORDER.get((kind, part), ())))

    def later(part):
        if part == 0:
            return owns[0][-1]
        first_sent = halos[0] if shards == 1 else get("meet", 0)[1]
        made = later_call(
            sizes, shards, part, blade_counts, orders, planes,
            known.get(("held", part), held), table, band, ready("later", part, first_sent),
        )
        owns.append(made[:shards])
        known["synthesis", 0] = made[shards]
        known["held", part + 1] = made[-1]
        return made[0]

    def halo(part):
        return exchange(ready("halo", part, halos[part]), "span", 1)

    def with_halo(part, k, *terms):
        get("later", part)
        total = jnp.where(holds[k], get("halo", part).astype(jnp.float32), 0.0)
        for term in (owns[part][k], *terms):
            total = total + term.astype(jnp.float32)
        return total.astype(jnp.bfloat16)

    def meet(part):
        return None, with_halo(part, 2)

    def pair_sent(part):
        sent = [get("meet", part)[1]]
        if JOIN == 2:
            sent.append(with_halo(part, 1))
        elif part > 0 and JOIN:
            sent.append(with_halo(part - 1, 1))
        return exchange(ready("pair", part, jnp.stack(sent)), "pitch", 1)

    def pair(part):
        return get("pair_sent", part)[0]

    def beside(part):
        if JOIN == 2:
            return get("pair_sent", part)[1]
        if part + 1 < instances and JOIN:
            return get("pair_sent", part + 1)[1]
        return exchange(ready("beside", part, with_halo(part, 1)), "pitch", 1)

    def across(part):
        return exchange(
            ready("across", part, with_halo(part, 3, get("pair", part))), "pitch", 3
        )

    def total(part):
        return with_halo(part, 0, get("beside", part), get("across", part))

    def spread(value, k):
        pairs = [
            (g * pitch_count + z, ((g + shift) % row_count) * pitch_count + (z ^ k))
            for g in range(row_count)
            for z in range(pitch_count)
        ]
        return lax.ppermute(value, ("row", "pitch"), pairs)

    def swap(part):
        return spread(ready("swap", part, get("total", part)), 0)

    def swap_across(part):
        return spread(ready("swap_across", part, get("total", part)), 3)

    def swap_beside(part):
        if part in DIRECT:
            return spread(ready("swap_beside", part, get("total", part)), 1)
        return exchange(ready("swap_beside", part, get("swap", part)), "pitch", 1)

    def across_on(part):
        return exchange(ready("across_on", part, get("swap_across", part)), "pitch", 1)

    def synth(at):
        base = get("synth", at - 1) if at else None
        group = {(part, k): get(names[k], part) for part, k in GROUPS[at]}
        return synthesise_call(count, shards, known["synthesis", 0], group, base)

    steps = dict(
        synth=synth,
        later=later, halo=halo, meet=meet, pair_sent=pair_sent, pair=pair, beside=beside, across=across, total=total,
        swap=swap, swap_across=swap_across, swap_beside=swap_beside, across_on=across_on,
    )
    names = ("swap", "swap_beside", "across_on", "swap_across")

    def whole_sum(part):
        get("later", part)
        wide = get("halo", part).astype(jnp.float32)
        low = jnp.pad(wide, ((0, 0), (rs_loc - halo_rows, 0), (0, 0)))
        high = jnp.pad(wide, ((0, 0), (0, rs_loc - halo_rows), (0, 0)))
        mine = owns[part][0] + jnp.where(lax.axis_index("span") == 0, low, high)
        return lax.psum(mine, "pitch").astype(jnp.bfloat16)

    joined = None
    get("later", instances - 1)
    if by_shards:
        joined = get("synth", len(GROUPS) - 1)
    else:
        pairs = [(g, (g + shift) % row_count) for g in range(row_count)]
        pieces = {
            (part, 0): lax.ppermute(whole_sum(part), "row", pairs) for part in range(instances)
        }
        joined = synthesise_call(count, shards, known["synthesis", 0], pieces, joined)
    return joined.reshape(1, instances, fields, rs_loc, pitch)


def solution(mesh):
    placed = (P("row", None, None, "span", "pitch"), P("span", None), P(), P(), P())
    return jax.shard_map(
        body,
        mesh=mesh,
        in_specs=placed,
        out_specs=P("row", None, None, "span", "pitch"),
        check_vma=False,
    )
```
